32 devices in a mesh: wide: 16 (over z, y, x), narrow: 2 (over core).
Axes of the slice: x: 2, y: 2, z: 4, core: 2. Of those that a mesh axis runs over, the one named last changes fastest.
Arguments:
- orbitals: float32 [112, 14, 7, 512], P('wide', 'narrow'), may hold values from -6 to 6
- cell_matrix: bfloat16 [16, 2, 1, 512, 512], P('wide', 'narrow'), as said below
- cell_order: int32 [16, 2, 1, 512], P('wide', 'narrow'), may hold values from 0 to 511, as said below
Outputs:
- filtered_basis: float32 [112, 14, 7, 512], P('wide', 'narrow')
The draws below stay inside these ranges and needn't reach their ends.
Inputs may be any that keep to these rules, and one draw needn't show every extreme that they name: Each row of cell_order lists the 512 cell node numbers of one cell in the order given by one of the 48 rotations and reflections of the cube. `cell_matrix`: each cell's matrix is symmetric.
All inputs are finite; a program needn't handle non-finite values.
Results may differ from the reference program's by a relative error of at most 0.00045.
The reference program's roundings to bfloat16 on the way count: a program that leaves them out, or rounds other values in their place, can miss the bound.
Values sent between devices are 32-bit elements; how exact they have to be, the bound alone decides.
No kernel may reach another device: no remote copies, remote signals or barrier semaphores. Data moves between devices by JAX's collectives and lax.ppermute only.
A program may use at most 64 MiB of HBM per device.

```python
import math
import jax
import jax.numpy as jnp
from jax import lax

ORDER = 7
PE = 8
CELLN = 512
NB = 512
C = 1
DEG = 4
ZN = 7
CELLS_X = 16
CELLS_Y = 2
GX = 112
GY = 14
NODES = 10976


def draw_cell_matrix(key, part):
    array_shape = (CELLS_X, CELLS_Y, C, CELLN, CELLN)
    key_one, key_two = jax.random.split(key)
    samples = jax.random.normal(key_one, array_shape, jnp.float32)
    diagonal = jax.random.uniform(key_two, array_shape[:-1], jnp.float32, 1.0, 2.0)
    symmetric = (samples + jnp.swapaxes(samples, -1, -2)) * (0.5 / math.sqrt(2.0 * CELLN))
    positions = jnp.arange(CELLN, dtype=jnp.int32)
    on_diagonal = positions[:, None] == positions[None, :]
    matrix_out = jnp.where(on_diagonal, diagonal[..., :, None], symmetric)
    return matrix_out.astype(jnp.bfloat16)


def draw_cell_order(key, part):
    cell_count = CELLS_X * CELLS_Y * C
    key_one, key_two = jax.random.split(key)
    axes_pick = jax.random.randint(key_one, (cell_count,), 0, 6)
    flip_bits = jax.random.randint(key_two, (cell_count, 3), 0, 2)
    symmetry_table = jnp.array([[0, 1, 2], [0, 2, 1], [1, 0, 2], [1, 2, 0], [2, 0, 1], [2, 1, 0]], dtype=jnp.int32)
    selected = symmetry_table[axes_pick]
    positions = jnp.arange(CELLN, dtype=jnp.int32)
    coordinates = jnp.stack([positions // (PE * PE), positions // PE % PE, positions % PE], axis=-1)
    spread = jnp.broadcast_to(coordinates[None], (cell_count, CELLN, 3))
    picked = jnp.take_along_axis(spread, jnp.broadcast_to(selected[:, None, :], (cell_count, CELLN, 3)), axis=2)
    flipped = jnp.where(flip_bits[:, None, :] == 1, PE - 1 - picked, picked)
    number = flipped[..., 0] * PE * PE + flipped[..., 1] * PE + flipped[..., 2]
    return number.reshape(CELLS_X, CELLS_Y, C, CELLN).astype(jnp.int32)


def block_scale(key, shape, cuts, least, high):
    def one(dim, shards_of):
        heights = jax.random.uniform(jax.random.fold_in(jax.random.fold_in(key, 6), dim), (shards_of,), jnp.float32, least / len(cuts), high / len(cuts))
        return jnp.repeat(jnp.exp(heights), shape[dim] // shards_of).reshape((-1,) + (1,) * (len(shape) - dim - 1))

    loudness = one(*cuts[0])
    for cut in cuts[1:]:
        loudness = loudness * one(*cut)
    return loudness


def noise(rng, shape, scale, bound, cuts=(), held_as=jnp.bfloat16):
    values = jax.random.normal(rng, shape, jnp.float32) * scale
    if len(cuts) > 0:
        values = block_scale(rng, shape, cuts, -0.22, 0.18) * values
    return jnp.clip(values, min=-bound, max=bound).astype(held_as)


def setup_inputs(seed: int = 0) -> dict:
    splits = jax.random.split(jax.random.key(seed), 4)
    orbitals = noise(splits[0], (GX, GY, ZN, NB), 1.0, 6.0, ((0, 16), (1, 2)), jnp.float32)
    cell_matrix = draw_cell_matrix(jax.random.fold_in(splits[3], 71), 0)
    cell_order = draw_cell_order(jax.random.fold_in(splits[3], 71), 0)
    return dict(orbitals=orbitals, cell_matrix=cell_matrix, cell_order=cell_order)


band_low = 4.0
band_high = 34.0
anchor = 0.0

def apply_cells(vector, matrices, cell_order, inverse_order):
    z_window = (ORDER * jnp.arange(C, dtype=jnp.int32)[:, None] + jnp.arange(PE, dtype=jnp.int32)[None, :]) % ZN
    y_window = (ORDER * jnp.arange(CELLS_Y, dtype=jnp.int32)[:, None] + jnp.arange(PE, dtype=jnp.int32)[None, :]) % GY

    def one_column(carry, column):
        x_window = (ORDER * column + jnp.arange(PE, dtype=jnp.int32)) % GX
        x_slab = jnp.take(vector, x_window, axis=0)
        cell_boxes = x_slab[:, y_window][:, :, :, z_window]
        cell_boxes = jnp.transpose(cell_boxes, (1, 3, 0, 2, 4, 5)).reshape(CELLS_Y, C, CELLN, NB)
        rounded = lax.optimization_barrier(cell_boxes.astype(jnp.bfloat16)).astype(jnp.float32)
        ordering = lax.dynamic_index_in_dim(cell_order, column, 0, keepdims=False)
        inverse_now = lax.dynamic_index_in_dim(inverse_order, column, 0, keepdims=False)
        matrices_f = lax.dynamic_index_in_dim(matrices, column, 0, keepdims=False).astype(jnp.float32)
        gathered = jnp.take_along_axis(rounded, ordering[..., None], axis=2)
        products = jnp.einsum('jckm,jcmn->jckn', matrices_f, gathered, precision=lax.Precision.HIGHEST)
        placed = jnp.take_along_axis(products, inverse_now[..., None], axis=2)
        placed = placed.reshape(CELLS_Y, C, PE, PE, PE, NB)
        placed = jnp.transpose(placed, (2, 0, 3, 1, 4, 5))
        carry = carry.at[x_window[:, None, None, None, None], y_window[None, :, :, None, None], z_window[None, None, None, :, :]].add(placed)
        return (carry, None)
    start = jnp.zeros(vector.shape, jnp.float32)
    result, _ = lax.scan(one_column, start, jnp.arange(CELLS_X, dtype=jnp.int32))
    return result

def reference(orbitals, cell_matrix, cell_order):
    inverse_order = jnp.argsort(cell_order, axis=-1).astype(jnp.int32)
    center = (band_low + band_high) / 2.0
    half_width = (band_high - band_low) / 2.0
    sigma_now = half_width / (anchor - center)
    tau_value = 2.0 / sigma_now

    def shifted_h(vector):
        return apply_cells(vector, cell_matrix, cell_order, inverse_order) - center * vector
    previous = orbitals
    current = shifted_h(previous) * (sigma_now / half_width)
    for degree_step in range(DEG - 1):
        sigma_new = 1.0 / (tau_value - sigma_now)
        updated = shifted_h(current) * (2.0 * sigma_new / half_width) - sigma_now * sigma_new * previous
        previous, current = (current, updated)
        sigma_now = sigma_new
    flattened = current.reshape(-1, NB)
    correlation = jnp.einsum('kn,km->nm', flattened, flattened, precision=lax.Precision.HIGHEST) / NODES
    lower_factor = jnp.linalg.cholesky(correlation)
    identity_matrix = jnp.eye(NB, dtype=jnp.float32)
    r_inverse = lax.linalg.triangular_solve(lower_factor, identity_matrix, left_side=True, lower=True).T
    result = jnp.dot(flattened, r_inverse, precision=lax.Precision.HIGHEST)
    return result.reshape(current.shape)
```

```python
import functools

import jax
import jax.numpy as jnp
from jax import lax
from jax.experimental import pallas as pl
from jax.experimental.pallas import tpu as pltpu
from jax.sharding import PartitionSpec as P

DEG = 4
SUB = 8
LANES = 128


band_low = 4.0
band_high = 34.0
anchor = 0.0


def vmem_call(body, out_shapes, scratch=(), flops=0):
    def call(*operands):
        return pl.pallas_call(
            body,
            out_shape=out_shapes,
            in_specs=[pl.BlockSpec(memory_space=pltpu.VMEM)] * len(operands),
            out_specs=jax.tree.map(
                lambda _: pl.BlockSpec(memory_space=pltpu.VMEM), out_shapes
            ),
            scratch_shapes=list(scratch),
            compiler_params=pltpu.CompilerParams(vmem_limit_bytes=32 << 20),
            cost_estimate=pl.CostEstimate(
                flops=flops, bytes_accessed=1 << 20, transcendentals=0
            ),
        )(*operands)

    return call


def f32(*shape):
    return jax.ShapeDtypeStruct(shape, jnp.float32)


def exact_dot(a, b, dims=((1,), (0,))):
    return lax.dot_general(
        a,
        b,
        (dims, ((), ())),
        precision=lax.Precision.HIGHEST,
        preferred_element_type=jnp.float32,
    )


def permute_body(matrix, order, out):
    count = matrix.shape[0]
    pick = (
        lax.broadcasted_iota(jnp.int32, (count, count), 1) == order[...]
    ).astype(jnp.bfloat16)
    half = lax.dot_general(
        matrix[...],
        pick,
        (((1,), (0,)), ((), ())),
        preferred_element_type=jnp.float32,
    ).astype(jnp.bfloat16)
    out[...] = lax.dot_general(
        half, pick, (((0,), (0,)), ((), ())), preferred_element_type=jnp.float32
    ).astype(jnp.bfloat16)


def cell_product(values, matrix, image, faces):
    edge = values.shape[0]
    width = values.shape[3]
    rows = values.reshape(edge**3, width).astype(jnp.bfloat16)
    products = jnp.dot(matrix[...], rows, preferred_element_type=jnp.float32)
    products = products.reshape(edge, edge, edge, width)
    wrap = products[:, :, :1] + products[:, :, edge - 1 :]
    where = lax.broadcasted_iota(jnp.int32, products.shape, 2)
    products = jnp.where((where == 0) | (where == edge - 1), wrap, products)
    image[...] = products
    faces[0] = products[:, 0]
    faces[1] = products[:, edge - 1]


def first_body(own, x_next, y_next, matrix, values, image, faces):
    order_now = own.shape[0]
    values[:order_now, :order_now, :order_now] = own[...]
    values[order_now:, :order_now, :order_now] = x_next[...]
    values[:, order_now:, :order_now] = y_next[...]
    values[:, :, order_now:] = values[:, :, :1]
    cell_product(values[...], matrix, image, faces)


def updated(image, y_faces, x_low, x_high, current, previous, alpha, beta):
    center = (band_low + band_high) / 2.0
    edge = image.shape[0]
    image[:, 0] = image[:, 0] + y_faces[0]
    if y_faces.shape[0] > 1:
        image[:, edge - 1] = image[:, edge - 1] + y_faces[1]
    image[0] = image[0] + x_low[...]
    if x_high is not None:
        image[edge - 1] = image[edge - 1] + x_high[...]
    got = (image[...] - center * current[...]) * alpha
    if previous is not None:
        got = got - beta * previous[...]
    return got


def middle_body(*refs, alpha, beta):
    if beta is None:
        image_in, y_faces, x_low, x_high, current, matrix, values, image, faces, work = refs
        previous = None
    else:
        image_in, y_faces, x_low, x_high, current, previous, matrix, values, image, faces, work = refs
    work[...] = image_in[...]
    got = updated(work, y_faces, x_low, x_high, current, previous, alpha, beta)
    values[...] = got
    cell_product(got, matrix, image, faces)


def last_body(image_in, y_face, x_low, current, previous, own, corr, work, *, alpha, beta):
    edge = image_in.shape[0]
    width = image_in.shape[3]
    work[...] = image_in[...]
    got = updated(work, y_face, x_low, None, current, previous, alpha, beta)
    got = got[: edge - 1, : edge - 1]
    where = lax.broadcasted_iota(jnp.int32, got.shape, 2)
    got = jnp.where(where == edge - 1, 0.0, got)
    flat = got.reshape((edge - 1) ** 2 * edge, width)
    own[...] = flat
    at = 0
    for j in range(0, width, LANES):
        block = exact_dot(flat[:, j:], flat[:, j : j + LANES], ((0,), (0,)))
        corr[at : at + width - j] = block
        at += width - j


def swap(block, axis, distance):
    count = lax.axis_size(axis)
    return lax.ppermute(block, axis, [(i, i ^ distance) for i in range(count)])


def stages_of(axis, size):
    stages, stride = [], 1
    while stride < size:
        radix = 4 if size // stride >= 4 else 2
        stages.append((axis, stride, radix))
        stride *= radix
    return stages


def summed(block):
    rows, lanes = block.shape
    stages = stages_of("narrow", lax.axis_size("narrow")) + stages_of(
        "wide", lax.axis_size("wide")
    )
    cut = 1
    for _, _, radix in stages[:-1]:
        cut *= radix
    padded = -(-rows // (cut * SUB)) * cut * SUB
    if padded != rows:
        block = jnp.pad(block, ((0, padded - rows), (0, 0)))
    for axis, stride, radix in stages[:-1]:
        mine = lax.axis_index(axis) // stride % radix
        parts = block.reshape(radix, -1, lanes)
        total = lax.dynamic_index_in_dim(parts, mine, 0, False)
        for d in range(1, radix):
            sent = lax.dynamic_index_in_dim(parts, mine ^ d, 0, False)
            total = total + swap(sent, axis, d * stride)
        block = total
    axis, stride, radix = stages[-1]
    got = [block] + [swap(block, axis, d * stride) for d in range(1, radix)]
    while len(got) > 1:
        got = [a + b for a, b in zip(got[::2], got[1::2])]
    block = got[0]
    for axis, stride, radix in reversed(stages[:-1]):
        mine = lax.axis_index(axis) // stride % radix
        parts = jnp.zeros((radix,) + block.shape, block.dtype)
        parts = lax.dynamic_update_index_in_dim(parts, block, mine, 0)
        for d in range(1, radix):
            parts = lax.dynamic_update_index_in_dim(
                parts, swap(block, axis, d * stride), mine ^ d, 0
            )
        block = parts.reshape(-1, lanes)
    return block[:rows]


def lane_spread(tile, column):
    return jnp.broadcast_to(tile[:, column : column + 1], tile.shape)


def row_spread(tile, row):
    return jnp.broadcast_to(tile[row : row + 1, :], tile.shape)


def inverse_factor(block):
    size = block.shape[0]
    steps = size // SUB
    left = [block[SUB * t : SUB * (t + 1)] for t in range(steps)]
    rows = lax.broadcasted_iota(jnp.int32, (SUB, size), 0)
    cols = lax.broadcasted_iota(jnp.int32, (SUB, size), 1)
    right = [
        jnp.where(cols == rows + SUB * t, 1.0, 0.0).astype(jnp.float32)
        for t in range(steps)
    ]
    done = []
    for s in range(steps):
        base = SUB * s
        spread = [lane_spread(left[s], base + d) for d in range(SUB)]
        a = {
            (c, d): row_spread(spread[d], c)
            for d in range(SUB)
            for c in range(d, SUB)
        }
        scale, low = [], {}
        for k in range(SUB):
            scale.append(lax.rsqrt(a[k, k]))
            for c in range(k + 1, SUB):
                low[c, k] = a[c, k] * scale[k]
            for d in range(k + 1, SUB):
                for c in range(d, SUB):
                    a[c, d] = a[c, d] - low[c, k] * low[d, k]

        def forward(tile):
            got = []
            for k in range(SUB):
                row = row_spread(tile, k)
                for m in range(k):
                    row = row - low[k, m] * got[m]
                got.append(row * scale[k])
            return got

        def backward(got):
            back = [None] * SUB
            for k in reversed(range(SUB)):
                row = got[k]
                for m in range(k + 1, SUB):
                    row = row - low[m, k] * back[m]
                back[k] = row * scale[k]
            return back

        inverse = forward(right[s])
        packed = inverse[0]
        for k in range(1, SUB):
            packed = jnp.where(rows == k, inverse[k], packed)
        done.append(packed)
        if s + 1 == steps:
            break
        upper = forward(left[s])
        t = s + 1
        factors = []
        for k in range(SUB):
            column = lane_spread(left[t], base + k)
            for m in range(k):
                column = column - factors[m] * low[k, m]
            factors.append(column * scale[k])
        for k in range(SUB):
            left[t] = left[t] - factors[k] * upper[k]
            right[t] = right[t] - factors[k] * inverse[k]
        if s + 2 < steps:
            upper, inverse = backward(upper), backward(inverse)
        for t in range(s + 2, steps):
            raw = [lane_spread(left[t], base + k) for k in range(SUB)]
            for k in range(SUB):
                left[t] = left[t] - raw[k] * upper[k]
                right[t] = right[t] - raw[k] * inverse[k]
    return jnp.concatenate(done, axis=0)


def ortho_body(corr, own, out, lower, rest, *, scale):
    width = own.shape[1]
    count = width // LANES
    at = 0
    for j in range(0, width, LANES):
        lower[j:, j : j + LANES] = corr[at : at + width - j] * scale
        at += width - j
    rest[...] = own[...]
    for k in range(count):
        begin, end = LANES * k, LANES * (k + 1)
        inverse = inverse_factor(lower[begin:end, begin:end])
        block = exact_dot(rest[:, begin:end], inverse, ((1,), (1,)))
        out[:, :, begin:end] = block.reshape(out.shape[0], SUB, LANES)[:, : SUB - 1]
        if k + 1 < count:
            under = exact_dot(lower[end:, begin:end], inverse, ((1,), (1,)))
            lower[end:, end:] = lower[end:, end:] - exact_dot(
                under, under, ((1,), (1,))
            )
            rest[:, end:] = rest[:, end:] - exact_dot(block, under, ((1,), (1,)))


def to_next(block, axis, distance):
    count = lax.axis_size(axis)
    return lax.ppermute(block, axis, [(i, (i + distance) % count) for i in range(count)])


def y_exchange(faces):
    if lax.axis_size("narrow") == 2:
        return to_next(faces[::-1], "narrow", 1)
    return jnp.stack([to_next(faces[1], "narrow", 1), to_next(faces[0], "narrow", -1)])


def with_faces(plane, y_faces, x_at):
    low = plane[:1] + y_faces[0, x_at][None]
    high = plane[-1:] + y_faces[1, x_at][None]
    return jnp.concatenate([low, plane[1:-1], high], axis=0)


def on_device(orbitals, cell_matrix, cell_order):
    order_now = orbitals.shape[0]
    edge = order_now + 1
    width = orbitals.shape[3]
    box = f32(edge, edge, edge, width)
    faces_shape = f32(2, edge, edge, width)
    cell_nodes = edge**3
    matrix = vmem_call(
        permute_body,
        jax.ShapeDtypeStruct((cell_nodes, cell_nodes), jnp.bfloat16),
        flops=4 * cell_nodes**3,
    )(
        cell_matrix.reshape(cell_nodes, cell_nodes),
        cell_order.reshape(cell_nodes, 1),
    )

    x_next = to_next(orbitals[:1], "wide", -1)
    first_rows = jnp.concatenate([orbitals[:, :1], x_next[:, :1]], axis=0)
    y_next = to_next(first_rows, "narrow", -1)
    product_flops = 2 * cell_nodes**2 * width
    current, image, faces = vmem_call(
        first_body, (box, box, faces_shape), flops=product_flops
    )(orbitals, x_next, y_next, matrix)

    half_width = (band_high - band_low) / 2.0
    sigma_now = half_width / (anchor - (band_low + band_high) / 2.0)
    tau_value = 2.0 / sigma_now
    alpha, beta, previous = sigma_now / half_width, None, None
    for degree_step in range(1, DEG):
        y_faces = y_exchange(faces)
        x_low = to_next(with_faces(image[edge - 1], y_faces, edge - 1), "wide", 1)
        x_high = to_next(with_faces(image[0], y_faces, 0), "wide", -1)
        operands = [image, y_faces, x_low, x_high, current]
        if previous is not None:
            operands.append(previous)
        next_values, image, faces = vmem_call(
            functools.partial(middle_body, alpha=alpha, beta=beta),
            (box, box, faces_shape),
            scratch=[pltpu.VMEM(box.shape, jnp.float32)],
            flops=product_flops,
        )(*operands, matrix)
        previous, current = current, next_values
        sigma_new = 1.0 / (tau_value - sigma_now)
        alpha, beta = 2.0 * sigma_new / half_width, sigma_now * sigma_new
        sigma_now = sigma_new

    y_low = to_next(faces[1:], "narrow", 1)
    last_plane = image[edge - 1]
    last_plane = jnp.concatenate(
        [last_plane[:1] + y_low[0, edge - 1][None], last_plane[1:]], axis=0
    )
    x_low = to_next(last_plane, "wide", 1)
    blocks = width // LANES
    own, corr = vmem_call(
        functools.partial(last_body, alpha=alpha, beta=beta),
        (
            f32(order_now**2 * edge, width),
            f32(blocks * (blocks + 1) // 2 * LANES, LANES),
        ),
        scratch=[pltpu.VMEM(box.shape, jnp.float32)],
        flops=2 * cell_nodes * width**2,
    )(image, y_low, x_low, current, previous)

    nodes = order_now**3 * lax.axis_size("wide") * lax.axis_size("narrow")
    corr = summed(corr)
    out = vmem_call(
        functools.partial(ortho_body, scale=1.0 / nodes),
        f32(order_now**2, order_now, width),
        scratch=[
            pltpu.VMEM((width, width), jnp.float32),
            pltpu.VMEM(own.shape, jnp.float32),
        ],
        flops=width**3,
    )(corr, own)
    return out.reshape(orbitals.shape)


def solution(mesh):
    return jax.shard_map(
        on_device,
        mesh=mesh,
        in_specs=(
            P("wide", "narrow", None, None),
            P("wide", "narrow", None, None, None),
            P("wide", "narrow", None, None),
        ),
        out_specs=P("wide", "narrow", None, None),
        check_vma=False,
    )
```

```python
import functools

import jax
import jax.numpy as jnp
from jax import lax
from jax.experimental import pallas as pl
from jax.experimental.pallas import tpu as pltpu
from jax.sharding import PartitionSpec as P

DEG = 4
SUB = 8
LANES = 128
VMEM_LIMIT = 8 << 20


band_low = 4.0
band_high = 34.0
anchor = 0.0


def vmem_call(body, out_shapes, scratch=(), flops=0):
    def call(*operands):
        return pl.pallas_call(
            body,
            out_shape=out_shapes,
            in_specs=[pl.BlockSpec(memory_space=pltpu.VMEM)] * len(operands),
            out_specs=jax.tree.map(
                lambda _: pl.BlockSpec(memory_space=pltpu.VMEM), out_shapes
            ),
            scratch_shapes=list(scratch),
            compiler_params=pltpu.CompilerParams(vmem_limit_bytes=VMEM_LIMIT),
            cost_estimate=pl.CostEstimate(
                flops=flops, bytes_accessed=1 << 20, transcendentals=0
            ),
        )(*operands)

    return call


def f32(*shape):
    return jax.ShapeDtypeStruct(shape, jnp.float32)


def exact_dot(a, b, dims=((1,), (0,))):
    return lax.dot_general(
        a,
        b,
        (dims, ((), ())),
        precision=lax.Precision.HIGHEST,
        preferred_element_type=jnp.float32,
    )


def permute_body(matrix, order, out):
    count = matrix.shape[0]
    pick = (
        lax.broadcasted_iota(jnp.int32, (count, count), 1) == order[...]
    ).astype(jnp.bfloat16)
    half = lax.dot_general(
        matrix[...],
        pick,
        (((1,), (0,)), ((), ())),
        preferred_element_type=jnp.float32,
    ).astype(jnp.bfloat16)
    out[...] = lax.dot_general(
        half, pick, (((0,), (0,)), ((), ())), preferred_element_type=jnp.float32
    ).astype(jnp.bfloat16)


def cell_product(values, matrix, image, x_first, x_last, y_sent):
    edge = values.shape[0]
    width = values.shape[3]
    rows = values.reshape(edge**3, width).astype(jnp.bfloat16)
    products = jnp.dot(matrix[...], rows, preferred_element_type=jnp.float32)
    products = products.reshape(edge, edge, edge, width)
    wrap = products[:, :, :1] + products[:, :, edge - 1 :]
    where = lax.broadcasted_iota(jnp.int32, products.shape, 2)
    products = jnp.where((where == 0) | (where == edge - 1), wrap, products)
    image[...] = products
    x_first[...] = products[0]
    x_last[...] = products[edge - 1]
    y_sent[0] = products[:, edge - 1]
    y_sent[1] = products[:, 0]


def first_body(own, x_next, y_next, corner, matrix, values, *sums):
    order_now = own.shape[0]
    values[:order_now, :order_now, :order_now] = own[...]
    values[order_now:, :order_now, :order_now] = x_next[...]
    values[:order_now, order_now:, :order_now] = y_next[...]
    values[order_now:, order_now:, :order_now] = corner[...]
    values[:, :, order_now:] = values[:, :, :1]
    cell_product(values[...], matrix, *sums)


def edge_body(*refs):
    *planes, y_faces = refs[: len(refs) // 2 + 1]
    outs = refs[len(refs) // 2 + 1 :]
    edge = planes[0].shape[0]
    for plane, out, at in zip(planes, outs, (edge - 1, 0)):
        out[...] = plane[...]
        out[0] = out[0] + y_faces[0, at]
        if y_faces.shape[0] > 1:
            out[edge - 1] = out[edge - 1] + y_faces[1, at]


def updated(image, y_faces, x_low, x_high, current, previous, alpha, beta):
    center = (band_low + band_high) / 2.0
    edge = image.shape[0]
    image[:, 0] = image[:, 0] + y_faces[0]
    if y_faces.shape[0] > 1:
        image[:, edge - 1] = image[:, edge - 1] + y_faces[1]
    image[0] = image[0] + x_low[...]
    if x_high is not None:
        image[edge - 1] = image[edge - 1] + x_high[...]
    got = (image[...] - center * current[...]) * alpha
    if previous is not None:
        got = got - beta * previous[...]
    return got


def middle_body(*refs, alpha, beta):
    if beta is None:
        image_in, y_faces, x_low, x_high, current, matrix, values, *sums, work = refs
        previous = None
    else:
        image_in, y_faces, x_low, x_high, current, previous, matrix, values, *sums, work = refs
    work[...] = image_in[...]
    got = updated(work, y_faces, x_low, x_high, current, previous, alpha, beta)
    values[...] = got
    cell_product(got, matrix, *sums)


def last_body(image_in, y_face, x_low, current, previous, own, corr, work, *, alpha, beta):
    edge = image_in.shape[0]
    width = image_in.shape[3]
    work[...] = image_in[...]
    got = updated(work, y_face, x_low, None, current, previous, alpha, beta)
    got = got[: edge - 1, : edge - 1]
    where = lax.broadcasted_iota(jnp.int32, got.shape, 2)
    got = jnp.where(where == edge - 1, 0.0, got)
    flat = got.reshape((edge - 1) ** 2 * edge, width)
    own[...] = flat
    at = 0
    for j in range(0, width, LANES):
        block = exact_dot(flat[:, j:], flat[:, j : j + LANES], ((0,), (0,)))
        corr[at : at + width - j] = block
        at += width - j


def swap(block, axis, distance):
    count = lax.axis_size(axis)
    return lax.ppermute(block, axis, [(i, i ^ distance) for i in range(count)])


def stages_of(axis, size):
    stages, stride = [], 1
    while stride < size:
        radix = 4 if size // stride >= 4 else 2
        stages.append((axis, stride, radix))
        stride *= radix
    return stages


def summed(block):
    rows, lanes = block.shape
    stages = stages_of("narrow", lax.axis_size("narrow")) + stages_of(
        "wide", lax.axis_size("wide")
    )
    cut = 1
    for _, _, radix in stages[:-1]:
        cut *= radix
    padded = -(-rows // (cut * SUB)) * cut * SUB
    if padded != rows:
        block = jnp.pad(block, ((0, padded - rows), (0, 0)))
    for axis, stride, radix in stages[:-1]:
        mine = lax.axis_index(axis) // stride % radix
        parts = block.reshape(radix, -1, lanes)
        total = lax.dynamic_index_in_dim(parts, mine, 0, False)
        for d in range(1, radix):
            sent = lax.dynamic_index_in_dim(parts, mine ^ d, 0, False)
            total = total + swap(sent, axis, d * stride)
        block = total
    axis, stride, radix = stages[-1]
    got = [block] + [swap(block, axis, d * stride) for d in range(1, radix)]
    while len(got) > 1:
        got = [a + b for a, b in zip(got[::2], got[1::2])]
    block = got[0]
    for axis, stride, radix in reversed(stages[:-1]):
        mine = lax.axis_index(axis) // stride % radix
        parts = jnp.zeros((radix,) + block.shape, block.dtype)
        parts = lax.dynamic_update_index_in_dim(parts, block, mine, 0)
        for d in range(1, radix):
            parts = lax.dynamic_update_index_in_dim(
                parts, swap(block, axis, d * stride), mine ^ d, 0
            )
        block = parts.reshape(-1, lanes)
    return block[:rows]


def lane_spread(tile, column):
    return jnp.broadcast_to(tile[:, column : column + 1], tile.shape)


def row_spread(tile, row):
    return jnp.broadcast_to(tile[row : row + 1, :], tile.shape)


def inverse_factor(block):
    size = block.shape[0]
    steps = size // SUB
    left = [block[SUB * t : SUB * (t + 1)] for t in range(steps)]
    rows = lax.broadcasted_iota(jnp.int32, (SUB, size), 0)
    cols = lax.broadcasted_iota(jnp.int32, (SUB, size), 1)
    right = [
        jnp.where(cols == rows + SUB * t, 1.0, 0.0).astype(jnp.float32)
        for t in range(steps)
    ]
    done = []
    for s in range(steps):
        base = SUB * s
        spread = [lane_spread(left[s], base + d) for d in range(SUB)]
        a = {
            (c, d): row_spread(spread[d], c)
            for d in range(SUB)
            for c in range(d, SUB)
        }
        scale, low = [], {}
        for k in range(SUB):
            scale.append(lax.rsqrt(a[k, k]))
            for c in range(k + 1, SUB):
                low[c, k] = a[c, k] * scale[k]
            for d in range(k + 1, SUB):
                for c in range(d, SUB):
                    a[c, d] = a[c, d] - low[c, k] * low[d, k]

        def forward(tile):
            got = []
            for k in range(SUB):
                row = row_spread(tile, k)
                for m in range(k):
                    row = row - low[k, m] * got[m]
                got.append(row * scale[k])
            return got

        def backward(got):
            back = [None] * SUB
            for k in reversed(range(SUB)):
                row = got[k]
                for m in range(k + 1, SUB):
                    row = row - low[m, k] * back[m]
                back[k] = row * scale[k]
            return back

        inverse = forward(right[s])
        packed = inverse[0]
        for k in range(1, SUB):
            packed = jnp.where(rows == k, inverse[k], packed)
        done.append(packed)
        if s + 1 == steps:
            break
        upper = forward(left[s])
        t = s + 1
        factors = []
        for k in range(SUB):
            column = lane_spread(left[t], base + k)
            for m in range(k):
                column = column - factors[m] * low[k, m]
            factors.append(column * scale[k])
        for k in range(SUB):
            left[t] = left[t] - factors[k] * upper[k]
            right[t] = right[t] - factors[k] * inverse[k]
        if s + 2 < steps:
            upper, inverse = backward(upper), backward(inverse)
        for t in range(s + 2, steps):
            raw = [lane_spread(left[t], base + k) for k in range(SUB)]
            for k in range(SUB):
                left[t] = left[t] - raw[k] * upper[k]
                right[t] = right[t] - raw[k] * inverse[k]
    return jnp.concatenate(done, axis=0)


def ortho_body(corr, own, out, lower, rest, *, scale):
    width = own.shape[1]
    count = width // LANES
    at = 0
    for j in range(0, width, LANES):
        lower[j:, j : j + LANES] = corr[at : at + width - j] * scale
        at += width - j
    rest[...] = own[...]
    for k in range(count):
        begin, end = LANES * k, LANES * (k + 1)
        inverse = inverse_factor(lower[begin:end, begin:end])
        block = exact_dot(rest[:, begin:end], inverse, ((1,), (1,)))
        out[:, :, begin:end] = block.reshape(out.shape[0], SUB, LANES)[:, : SUB - 1]
        if k + 1 < count:
            under = exact_dot(lower[end:, begin:end], inverse, ((1,), (1,)))
            lower[end:, end:] = lower[end:, end:] - exact_dot(
                under, under, ((1,), (1,))
            )
            rest[:, end:] = rest[:, end:] - exact_dot(block, under, ((1,), (1,)))


def to_next(block, axis, distance):
    count = lax.axis_size(axis)
    return lax.ppermute(block, axis, [(i, (i + distance) % count) for i in range(count)])


def from_next_both(block):
    rows, columns = lax.axis_size("wide"), lax.axis_size("narrow")
    route = [
        ((i + 1) % rows * columns + (j + 1) % columns, i * columns + j)
        for i in range(rows)
        for j in range(columns)
    ]
    return lax.ppermute(block, ("wide", "narrow"), route)


def y_exchange(sent):
    if lax.axis_size("narrow") == 2:
        return to_next(sent, "narrow", 1)
    return jnp.concatenate(
        [to_next(sent[:1], "narrow", 1), to_next(sent[1:], "narrow", -1)]
    )


def on_device(orbitals, cell_matrix, cell_order):
    order_now = orbitals.shape[0]
    edge = order_now + 1
    width = orbitals.shape[3]
    box = f32(edge, edge, edge, width)
    plane = f32(edge, edge, width)
    sums = (box, plane, plane, f32(2, edge, edge, width))
    cell_nodes = edge**3
    matrix = vmem_call(
        permute_body,
        jax.ShapeDtypeStruct((cell_nodes, cell_nodes), jnp.bfloat16),
        flops=4 * cell_nodes**3,
    )(
        cell_matrix.reshape(cell_nodes, cell_nodes),
        cell_order.reshape(cell_nodes, 1),
    )

    x_next = to_next(orbitals[:1], "wide", -1)
    corner = from_next_both(orbitals[:1, :1])
    y_next = to_next(orbitals[:, :1], "narrow", -1)
    product_flops = 2 * cell_nodes**2 * width
    current, image, x_first, x_last, y_sent = vmem_call(
        first_body, (box, *sums), flops=product_flops
    )(orbitals, x_next, y_next, corner, matrix)

    half_width = (band_high - band_low) / 2.0
    sigma_now = half_width / (anchor - (band_low + band_high) / 2.0)
    tau_value = 2.0 / sigma_now
    alpha, beta, previous = sigma_now / half_width, None, None
    for degree_step in range(1, DEG):
        y_faces = y_exchange(y_sent)
        x_last, x_first = vmem_call(edge_body, (plane, plane))(
            x_last, x_first, y_faces
        )
        x_low = to_next(x_last, "wide", 1)
        x_high = to_next(x_first, "wide", -1)
        operands = [image, y_faces, x_low, x_high, current]
        if previous is not None:
            operands.append(previous)
        next_values, image, x_first, x_last, y_sent = vmem_call(
            functools.partial(middle_body, alpha=alpha, beta=beta),
            (box, *sums),
            scratch=[pltpu.VMEM(box.shape, jnp.float32)],
            flops=product_flops,
        )(*operands, matrix)
        previous, current = current, next_values
        sigma_new = 1.0 / (tau_value - sigma_now)
        alpha, beta = 2.0 * sigma_new / half_width, sigma_now * sigma_new
        sigma_now = sigma_new

    y_low = to_next(y_sent[:1], "narrow", 1)
    (x_last,) = vmem_call(edge_body, (plane,))(x_last, y_low)
    x_low = to_next(x_last, "wide", 1)
    blocks = width // LANES
    own, corr = vmem_call(
        functools.partial(last_body, alpha=alpha, beta=beta),
        (
            f32(order_now**2 * edge, width),
            f32(blocks * (blocks + 1) // 2 * LANES, LANES),
        ),
        scratch=[pltpu.VMEM(box.shape, jnp.float32)],
        flops=2 * cell_nodes * width**2,
    )(image, y_low, x_low, current, previous)

    nodes = order_now**3 * lax.axis_size("wide") * lax.axis_size("narrow")
    corr = summed(corr)
    out = vmem_call(
        functools.partial(ortho_body, scale=1.0 / nodes),
        f32(order_now**2, order_now, width),
        scratch=[
            pltpu.VMEM((width, width), jnp.float32),
            pltpu.VMEM(own.shape, jnp.float32),
        ],
        flops=width**3,
    )(corr, own)
    return out.reshape(orbitals.shape)


def solution(mesh):
    return jax.shard_map(
        on_device,
        mesh=mesh,
        in_specs=(
            P("wide", "narrow", None, None),
            P("wide", "narrow", None, None, None),
            P("wide", "narrow", None, None),
        ),
        out_specs=P("wide", "narrow", None, None),
        check_vma=False,
    )
```

```python
import functools

import jax
import jax.numpy as jnp
from jax import lax
from jax.experimental import pallas as pl
from jax.experimental.pallas import tpu as pltpu
from jax.sharding import PartitionSpec as P

DEG = 4
SUB = 8
LANES = 128
SLAB = 16
STRIP = 256
PARTS = 1
VMEM_LIMIT = 6 << 20
LAST_LIMIT = 6 << 20
ORTHO_LIMIT = 6 << 20


band_low = 4.0
band_high = 34.0
anchor = 0.0


def vmem_call(body, out_shapes, scratch=(), flops=0, scalars=0, hbm_in=(), hbm_out=(), limit=VMEM_LIMIT):
    def spec(in_hbm):
        return pl.BlockSpec(memory_space=pltpu.HBM if in_hbm else pltpu.VMEM)

    def call(*operands):
        operands = [
            x
            if n < scalars
            else pltpu.with_memory_space_constraint(
                x, pltpu.HBM if n in hbm_in else pltpu.VMEM
            )
            for n, x in enumerate(operands)
        ]
        outs = tuple(
            (pltpu.HBM if n in hbm_out else pltpu.VMEM)(x.shape, x.dtype)
            for n, x in enumerate(out_shapes)
        )
        return pl.pallas_call(
            body,
            out_shape=outs,
            in_specs=[pl.BlockSpec(memory_space=pltpu.SMEM)] * scalars
            + [spec(n in hbm_in) for n in range(scalars, len(operands))],
            out_specs=tuple(spec(n in hbm_out) for n in range(len(out_shapes))),
            scratch_shapes=list(scratch),
            compiler_params=pltpu.CompilerParams(vmem_limit_bytes=limit),
            cost_estimate=pl.CostEstimate(
                flops=flops, bytes_accessed=1 << 20, transcendentals=0
            ),
        )(*operands)

    return call


def f32(*shape):
    return jax.ShapeDtypeStruct(shape, jnp.float32)


def exact_dot(a, b, dims=((1,), (0,))):
    return lax.dot_general(
        a,
        b,
        (dims, ((), ())),
        precision=lax.Precision.HIGHEST,
        preferred_element_type=jnp.float32,
    )


def permute_body(matrix, order, out):
    count = matrix.shape[0]
    pick = (
        lax.broadcasted_iota(jnp.int32, (count, count), 1) == order[...]
    ).astype(jnp.bfloat16)
    half = lax.dot_general(
        matrix[...],
        pick,
        (((1,), (0,)), ((), ())),
        preferred_element_type=jnp.float32,
    ).astype(jnp.bfloat16)
    out[...] = lax.dot_general(
        half, pick, (((0,), (0,)), ((), ())), preferred_element_type=jnp.float32
    ).astype(jnp.bfloat16)


def cell_product(values, matrix, image, x_first, x_last, y_sent):
    edge = values.shape[0]
    width = values.shape[3]
    rows = values.reshape(edge**3, width).astype(jnp.bfloat16)
    products = jnp.dot(matrix[...], rows, preferred_element_type=jnp.float32)
    products = products.reshape(edge, edge, edge, width)
    wrap = products[:, :, :1] + products[:, :, edge - 1 :]
    where = lax.broadcasted_iota(jnp.int32, products.shape, 2)
    products = jnp.where((where == 0) | (where == edge - 1), wrap, products)
    image[...] = products
    x_first[...] = products[0]
    x_last[...] = products[edge - 1]
    y_sent[0] = products[:, edge - 1]
    y_sent[1] = products[:, 0]


def first_body(own, x_next, y_next, corner, matrix, values, *sums):
    order_now = own.shape[0]
    values[:order_now, :order_now, :order_now] = own[...]
    values[order_now:, :order_now, :order_now] = x_next[...]
    values[:order_now, order_now:, :order_now] = y_next[...]
    values[order_now:, order_now:, :order_now] = corner[...]
    values[:, :, order_now:] = values[:, :, :1]
    cell_product(values[...], matrix, *sums)


def edge_body(*refs):
    *planes, y_faces = refs[: len(refs) // 2 + 1]
    outs = refs[len(refs) // 2 + 1 :]
    edge = planes[0].shape[0]
    for plane, out, at in zip(planes, outs, (edge - 1, 0)):
        out[...] = plane[...]
        out[0] = out[0] + y_faces[0, at]
        if y_faces.shape[0] > 1:
            out[edge - 1] = out[edge - 1] + y_faces[1, at]


def updated(image, y_faces, x_low, x_high, current, previous, alpha, beta):
    center = (band_low + band_high) / 2.0
    edge = image.shape[0]
    image[:, 0] = image[:, 0] + y_faces[0]
    if y_faces.shape[0] > 1:
        image[:, edge - 1] = image[:, edge - 1] + y_faces[1]
    image[0] = image[0] + x_low[...]
    if x_high is not None:
        image[edge - 1] = image[edge - 1] + x_high[...]
    got = (image[...] - center * current[...]) * alpha
    if previous is not None:
        got = got - beta * previous[...]
    return got


def middle_body(*refs, alpha, beta):
    if beta is None:
        image_in, y_faces, x_low, x_high, current, matrix, values, *sums, work = refs
        previous = None
    else:
        image_in, y_faces, x_low, x_high, current, previous, matrix, values, *sums, work = refs
    work[...] = image_in[...]
    got = updated(work, y_faces, x_low, x_high, current, previous, alpha, beta)
    values[...] = got
    cell_product(got, matrix, *sums)


def last_body(mine, image_in, y_face, x_low, current, previous, own, *refs, alpha, beta):
    *parts, corr, work, values, sem = refs
    edge = image_in.shape[0]
    width = image_in.shape[3]
    work[...] = image_in[...]
    got = updated(work, y_face, x_low, None, current, previous, alpha, beta)
    got = got[: edge - 1, : edge - 1]
    where = lax.broadcasted_iota(jnp.int32, got.shape, 2)
    got = jnp.where(where == edge - 1, 0.0, got)
    flat = got.reshape((edge - 1) ** 2 * edge, width)
    values[...] = flat
    keep = pltpu.make_async_copy(values, own, sem)
    keep.start()
    at = 0
    for i in range(0, width, STRIP):
        strip = exact_dot(flat[:, i : i + STRIP], flat[:, i:], ((0,), (0,)))
        for first in range(0, STRIP, LANES):
            for j in range(first, width - i, LANES):
                corr[at : at + LANES] = strip[first : first + LANES, j : j + LANES]
                at += LANES
    rows = parts[0].shape[0]
    for d, part in enumerate(parts):
        part[...] = corr[pl.ds(pl.multiple_of((mine[0] ^ d) * rows, SUB), rows)]
    keep.wait()


def swap(block, axis, distance):
    count = lax.axis_size(axis)
    return lax.ppermute(block, axis, [(i, i ^ distance) for i in range(count)])


def stages_of(axis, size):
    stages, stride = [], 1
    while stride < size:
        radix = 4 if size // stride >= 4 else 2
        stages.append((axis, stride, radix))
        stride *= radix
    return stages


def all_stages():
    return stages_of("narrow", lax.axis_size("narrow")) + stages_of(
        "wide", lax.axis_size("wide")
    )


def cut_rows(rows):
    cut = SUB
    for _, _, radix in all_stages()[:-1]:
        cut *= radix
    return -(-rows // cut) * cut


def cut_body(mine, *refs, count):
    terms, (*parts, work) = refs[:count], refs[count:]
    got = terms[0][...]
    for term in terms[1:]:
        got = got + term[...]
    work[...] = got
    rows = parts[0].shape[0]
    for d, part in enumerate(parts):
        part[...] = work[pl.ds(pl.multiple_of((mine[0] ^ d) * rows, SUB), rows)]


def digit(stage):
    axis, stride, radix = stage
    return (lax.axis_index(axis) // stride % radix).astype(jnp.int32)[None]


def summed(parts):
    lanes = parts[0].shape[1]
    stages = all_stages()
    for stage, after in zip(stages[:-1], stages[1:]):
        axis, stride, _ = stage
        terms = [swap(part, axis, d * stride) for d, part in enumerate(parts)]
        rows, radix = terms[0].shape[0], after[2]
        if after == stages[-1]:
            radix = 1
        parts = vmem_call(
            functools.partial(cut_body, count=len(terms)),
            (f32(rows // radix, lanes),) * radix,
            scratch=[pltpu.VMEM((rows, lanes), jnp.float32)],
            scalars=1,
        )(digit(after) if radix > 1 else jnp.zeros((1,), jnp.int32), *terms)
    block = parts[0]
    axis, stride, radix = stages[-1]
    got = [block] + [swap(block, axis, d * stride) for d in range(1, radix)]
    while len(got) > 1:
        got = [a + b for a, b in zip(got[::2], got[1::2])]
    block = got[0]
    for axis, stride, radix in reversed(stages[:-1]):
        mine = lax.axis_index(axis) // stride % radix
        parts = jnp.zeros((radix,) + block.shape, block.dtype)
        parts = lax.dynamic_update_index_in_dim(parts, block, mine, 0)
        for d in range(1, radix):
            parts = lax.dynamic_update_index_in_dim(
                parts, swap(block, axis, d * stride), mine ^ d, 0
            )
        block = parts.reshape(-1, lanes)
    return block


def lane_spread(tile, column):
    return jnp.broadcast_to(tile[:, column : column + 1], tile.shape)


def row_spread(tile, row):
    return jnp.broadcast_to(tile[row : row + 1, :], tile.shape)


def total(terms):
    while len(terms) > 1:
        terms = [a + b for a, b in zip(terms[::2], terms[1::2])]
    return terms[0]


def inverse_factor(block):
    size = block.shape[0]
    steps, per = size // SUB, SLAB // SUB
    tiles = [block[SUB * t : SUB * (t + 1)] for t in range(steps)]
    rows = lax.broadcasted_iota(jnp.int32, (SUB, size), 0)
    cols = lax.broadcasted_iota(jnp.int32, (SUB, size), 1)
    done = [None] * steps
    for s in range(0, steps, per):
        base = SUB * s
        own = (cols >= base) & (cols < base + SLAB)
        col = [
            {
                t: lane_spread(tiles[t], base + d)
                for t in range(s, s + per)
                if SUB * (t - s + 1) > d
            }
            for d in range(SLAB)
        ]
        before = list(tiles)
        for t in range(s, s + per):
            unit = jnp.where(cols == rows + SUB * t, 1.0, 0.0)
            tiles[t] = jnp.where(own, unit, tiles[t])
        for t in range(s + per, steps):
            tiles[t] = jnp.where(own, 0.0, tiles[t])

        def at(column, r):
            return row_spread(column[s + r // SUB], r % SUB)

        low, scale = [], []
        for k in range(0, SLAB, 2):
            x, y = col[k], col[k + 1]
            a, b, c = at(x, k), at(x, k + 1), at(y, k + 1)
            root = lax.rsqrt(a)
            next_root = lax.rsqrt(a * c - b * b)
            over = next_root * next_root
            p, q, u = {}, {}, {}
            for t in y:
                u[t] = a * y[t] - b * x[t]
                p[t] = (c * x[t] - b * y[t]) * over
                q[t] = u[t] * over
            for d in range(k + 2, SLAB):
                xd, yd = at(x, d), at(y, d)
                for t in col[d]:
                    col[d][t] = col[d][t] - (p[t] * xd + q[t] * yd)
            both = root * next_root
            here, r = s + k // SUB, k % SUB
            first = row_spread(tiles[here], r)
            second = row_spread(tiles[here], r + 1)
            for t in y:
                pm, qm = p[t], q[t]
                if t == here:
                    ratio = jnp.where(rows == r + 1, b * (root * root), 0.0)
                    pm = jnp.where(rows > r + 1, pm, ratio)
                    qm = jnp.where(rows > r + 1, qm, 0.0)
                tiles[t] = tiles[t] - (pm * first + qm * second)
            low.append({t: x[t] * root for t in y})
            low.append({t: u[t] * both for t in y})
            scale += [root, a * both]
        upper = []
        for i in range(per):
            t = s + i
            factors = scale[SUB * i]
            for k in range(1, SUB):
                factors = jnp.where(rows == k, scale[SUB * i + k], factors)
            tiles[t] = tiles[t] * factors
            done[t] = jnp.where(cols < base + SLAB, tiles[t], 0.0)
            upper += [row_spread(tiles[t], k) for k in range(SUB)]
        yield None
        if s + per < steps:
            solved = [None] * SLAB
            for k in reversed(range(SLAB)):
                row = upper[k]
                for m in reversed(range(k + 1, SLAB)):
                    row = row - at(low[k], m) * solved[m]
                solved[k] = row * scale[k]
            for t in range(s + per, steps):
                tiles[t] = tiles[t] - total(
                    [
                        lane_spread(before[t], base + k) * solved[k]
                        for k in reversed(range(SLAB))
                    ]
                )
    yield jnp.concatenate(done, axis=0)


def ortho_body(corr, own, out, blocks, rest, done, sent, sems, *, scale):
    width = own.shape[1]
    count = width // LANES
    nodes = own.shape[0]
    part = nodes // PARTS

    def span(k):
        return pl.ds(LANES * k, LANES)

    work = []

    def factored(block):
        share = -(-len(work) // (LANES // SLAB - 1))
        for got in inverse_factor(block):
            if got is None:
                for task in [work.pop(0) for _ in range(min(share, len(work)))]:
                    task()
        while work:
            work.pop(0)()
        return got

    place, at = {}, 0
    for i in range(count):
        for j in range(i, count):
            place[i, j] = at
            at += 1

    def piece(i, j):
        return corr[place[i, j] * LANES : (place[i, j] + 1) * LANES] * scale

    def set_up():
        for (i, j), n in place.items():
            if j > 0:
                blocks[n] = piece(i, j)
        rest[...] = own[...]

    def store(k):
        return pltpu.make_async_copy(sent.at[k], out.at[:, :, span(k)], sems.at[k])

    def finish(rows, k, block):
        done[rows, :] = block
        first, last = rows.start // SUB, rows.stop // SUB
        shaped = block.reshape(last - first, SUB, LANES)
        sent[k, first:last] = shaped[:, : SUB - 1]

    work.append(set_up)
    inverse = factored(piece(0, 0))
    for k in range(count - 1):
        near = exact_dot(inverse, blocks[place[k, k + 1]])
        diagonal = blocks[place[k + 1, k + 1]] - exact_dot(near, near, ((0,), (0,)))
        ups = {k + 1: near}

        def up_of(j, k=k, inverse=inverse, ups=ups):
            ups[j] = exact_dot(inverse, blocks[place[k, j]])

        def update(i, j, ups=ups):
            n = place[i, j]
            blocks[n] = blocks[n] - exact_dot(ups[i], ups[j], ((0,), (0,)))

        def solve(rows, k=k, inverse=inverse):
            finish(rows, k, exact_dot(rest[rows, span(k)], inverse, ((1,), (1,))))

        def subtract(rows, j, ups=ups):
            rest[rows, span(j)] = rest[rows, span(j)] - exact_dot(done[rows, :], ups[j])

        strips = [slice(r, r + part) for r in range(0, nodes, part)]
        later = range(k + 2, count)
        work += [functools.partial(up_of, j) for j in later]
        work += [
            functools.partial(update, i, j)
            for i in range(k + 1, count)
            for j in range(max(i, k + 2), count)
        ]
        work += [functools.partial(solve, rows) for rows in strips]
        work += [
            functools.partial(subtract, rows, j)
            for j in range(k + 1, count)
            for rows in strips
        ]
        inverse = factored(diagonal)
    last = count - 1
    finish(
        slice(0, nodes),
        last,
        exact_dot(rest[:, span(last)], inverse, ((1,), (1,))),
    )
    for k in range(count):
        store(k).start()
    for k in range(count):
        store(k).wait()


def to_next(block, axis, distance):
    count = lax.axis_size(axis)
    return lax.ppermute(block, axis, [(i, (i + distance) % count) for i in range(count)])


def from_next_both(block):
    rows, columns = lax.axis_size("wide"), lax.axis_size("narrow")
    route = [
        ((i + 1) % rows * columns + (j + 1) % columns, i * columns + j)
        for i in range(rows)
        for j in range(columns)
    ]
    return lax.ppermute(block, ("wide", "narrow"), route)


def y_exchange(sent):
    if lax.axis_size("narrow") == 2:
        return to_next(sent, "narrow", 1)
    return jnp.concatenate(
        [to_next(sent[:1], "narrow", 1), to_next(sent[1:], "narrow", -1)]
    )


def on_device(orbitals, cell_matrix, cell_order):
    order_now = orbitals.shape[0]
    edge = order_now + 1
    width = orbitals.shape[3]
    box = f32(edge, edge, edge, width)
    plane = f32(edge, edge, width)
    sums = (box, plane, plane, f32(2, edge, edge, width))
    cell_nodes = edge**3
    (matrix,) = vmem_call(
        permute_body,
        (jax.ShapeDtypeStruct((cell_nodes, cell_nodes), jnp.bfloat16),),
        flops=4 * cell_nodes**3,
    )(
        cell_matrix.reshape(cell_nodes, cell_nodes),
        cell_order.reshape(cell_nodes, 1),
    )

    x_next = to_next(orbitals[:1], "wide", -1)
    corner = from_next_both(orbitals[:1, :1])
    y_next = to_next(orbitals[:, :1], "narrow", -1)
    product_flops = 2 * cell_nodes**2 * width
    current, image, x_first, x_last, y_sent = vmem_call(
        first_body, (box, *sums), flops=product_flops
    )(orbitals, x_next, y_next, corner, matrix)

    half_width = (band_high - band_low) / 2.0
    sigma_now = half_width / (anchor - (band_low + band_high) / 2.0)
    tau_value = 2.0 / sigma_now
    alpha, beta, previous = sigma_now / half_width, None, None
    for degree_step in range(1, DEG):
        y_faces = y_exchange(y_sent)
        x_last, x_first = vmem_call(edge_body, (plane, plane))(
            x_last, x_first, y_faces
        )
        x_low = to_next(x_last, "wide", 1)
        x_high = to_next(x_first, "wide", -1)
        operands = [image, y_faces, x_low, x_high, current]
        if previous is not None:
            operands.append(previous)
        next_values, image, x_first, x_last, y_sent = vmem_call(
            functools.partial(middle_body, alpha=alpha, beta=beta),
            (box, *sums),
            scratch=[pltpu.VMEM(box.shape, jnp.float32)],
            flops=product_flops,
        )(*operands, matrix)
        previous, current = current, next_values
        sigma_new = 1.0 / (tau_value - sigma_now)
        alpha, beta = 2.0 * sigma_new / half_width, sigma_now * sigma_new
        sigma_now = sigma_new

    y_low = to_next(y_sent[:1], "narrow", 1)
    (x_last,) = vmem_call(edge_body, (plane,))(x_last, y_low)
    x_low = to_next(x_last, "wide", 1)
    blocks = width // LANES
    rows = cut_rows(blocks * (blocks + 1) // 2 * LANES)
    first_stage = all_stages()[0]
    radix = first_stage[2]
    own, *parts = vmem_call(
        functools.partial(last_body, alpha=alpha, beta=beta),
        (f32(order_now**2 * edge, width),) + (f32(rows // radix, LANES),) * radix,
        scratch=[
            pltpu.VMEM((rows, LANES), jnp.float32),
            pltpu.VMEM(box.shape, jnp.float32),
            pltpu.VMEM((order_now**2 * edge, width), jnp.float32),
            pltpu.SemaphoreType.DMA,
        ],
        flops=2 * cell_nodes * width**2,
        hbm_out=(0,),
        scalars=1,
        limit=LAST_LIMIT,
    )(digit(first_stage), image, y_low, x_low, current, previous)

    nodes = order_now**3 * lax.axis_size("wide") * lax.axis_size("narrow")
    corr = summed(parts)
    (out,) = vmem_call(
        functools.partial(ortho_body, scale=1.0 / nodes),
        (f32(order_now**2, order_now, width),),
        scratch=[
            pltpu.VMEM((corr.shape[0] // LANES, LANES, LANES), jnp.float32),
            pltpu.VMEM(own.shape, jnp.float32),
            pltpu.VMEM((own.shape[0], LANES), jnp.float32),
            pltpu.VMEM((blocks, order_now**2, order_now, LANES), jnp.float32),
            pltpu.SemaphoreType.DMA((blocks,)),
        ],
        flops=width**3,
        limit=ORTHO_LIMIT,
        hbm_out=(0,),
    )(corr, own)
    return out.reshape(orbitals.shape)


def solution(mesh):
    return jax.shard_map(
        on_device,
        mesh=mesh,
        in_specs=(
            P("wide", "narrow", None, None),
            P("wide", "narrow", None, None, None),
            P("wide", "narrow", None, None),
        ),
        out_specs=P("wide", "narrow", None, None),
        check_vma=False,
    )
```

```python
import functools

import jax
import jax.numpy as jnp
from jax import lax
from jax.experimental import pallas as pl
from jax.experimental.pallas import tpu as pltpu
from jax.sharding import PartitionSpec as P

DEG = 4
SUB = 8
LANES = 128
SLAB = 16
PARTS = 1
VMEM_LIMIT = 6 << 20


band_low = 4.0
band_high = 34.0
anchor = 0.0


def vmem_call(body, out_shapes, scratch=(), flops=0, scalars=0, hbm_in=(), hbm_out=()):
    def spec(in_hbm):
        return pl.BlockSpec(memory_space=pltpu.HBM if in_hbm else pltpu.VMEM)

    def call(*operands):
        operands = [
            x
            if n < scalars
            else pltpu.with_memory_space_constraint(
                x, pltpu.HBM if n in hbm_in else pltpu.VMEM
            )
            for n, x in enumerate(operands)
        ]
        outs = tuple(
            (pltpu.HBM if n in hbm_out else pltpu.VMEM)(x.shape, x.dtype)
            for n, x in enumerate(out_shapes)
        )
        return pl.pallas_call(
            body,
            out_shape=outs,
            in_specs=[pl.BlockSpec(memory_space=pltpu.SMEM)] * scalars
            + [spec(n in hbm_in) for n in range(scalars, len(operands))],
            out_specs=tuple(spec(n in hbm_out) for n in range(len(out_shapes))),
            scratch_shapes=list(scratch),
            compiler_params=pltpu.CompilerParams(vmem_limit_bytes=VMEM_LIMIT),
            cost_estimate=pl.CostEstimate(
                flops=flops, bytes_accessed=1 << 20, transcendentals=0
            ),
        )(*operands)

    return call


def f32(*shape):
    return jax.ShapeDtypeStruct(shape, jnp.float32)


def exact_dot(a, b, dims=((1,), (0,))):
    return lax.dot_general(
        a,
        b,
        (dims, ((), ())),
        precision=lax.Precision.HIGHEST,
        preferred_element_type=jnp.float32,
    )


def permute_body(matrix, order, out):
    count = matrix.shape[0]
    pick = (
        lax.broadcasted_iota(jnp.int32, (count, count), 1) == order[...]
    ).astype(jnp.bfloat16)
    half = lax.dot_general(
        matrix[...],
        pick,
        (((1,), (0,)), ((), ())),
        preferred_element_type=jnp.float32,
    ).astype(jnp.bfloat16)
    out[...] = lax.dot_general(
        half, pick, (((0,), (0,)), ((), ())), preferred_element_type=jnp.float32
    ).astype(jnp.bfloat16)


def cell_product(values, matrix, image, x_first, x_last, y_sent):
    edge = values.shape[0]
    width = values.shape[3]
    rows = values.reshape(edge**3, width).astype(jnp.bfloat16)
    products = jnp.dot(matrix[...], rows, preferred_element_type=jnp.float32)
    products = products.reshape(edge, edge, edge, width)
    wrap = products[:, :, :1] + products[:, :, edge - 1 :]
    where = lax.broadcasted_iota(jnp.int32, products.shape, 2)
    products = jnp.where((where == 0) | (where == edge - 1), wrap, products)
    image[...] = products
    x_first[...] = products[0]
    x_last[...] = products[edge - 1]
    y_sent[0] = products[:, edge - 1]
    y_sent[1] = products[:, 0]


def first_body(own, x_next, y_next, corner, matrix, values, *sums):
    order_now = own.shape[0]
    values[:order_now, :order_now, :order_now] = own[...]
    values[order_now:, :order_now, :order_now] = x_next[...]
    values[:order_now, order_now:, :order_now] = y_next[...]
    values[order_now:, order_now:, :order_now] = corner[...]
    values[:, :, order_now:] = values[:, :, :1]
    cell_product(values[...], matrix, *sums)


def edge_body(*refs):
    *planes, y_faces = refs[: len(refs) // 2 + 1]
    outs = refs[len(refs) // 2 + 1 :]
    edge = planes[0].shape[0]
    order_now = edge - 1
    for plane, out, at in zip(planes, outs, (edge - 1, 0)):
        for b in range(edge):
            row = plane[b]
            if b == 0:
                row = row + y_faces[0, at]
            if b == edge - 1 and y_faces.shape[0] > 1:
                row = row + y_faces[1, at]
            out[order_now * b : order_now * (b + 1)] = row[:order_now]


def updated(image, y_faces, x_low, x_high, current, previous, alpha, beta):
    center = (band_low + band_high) / 2.0
    edge = image.shape[0]
    image[:, 0] = image[:, 0] + y_faces[0]
    if y_faces.shape[0] > 1:
        image[:, edge - 1] = image[:, edge - 1] + y_faces[1]
    order_now = edge - 1
    for at, got in ((0, x_low), (edge - 1, x_high)):
        if got is not None:
            for b in range(edge):
                first = order_now * b
                image[at, b, :order_now] += got[first : first + order_now]
                image[at, b, order_now:] += got[first : first + 1]
    got = (image[...] - center * current[...]) * alpha
    if previous is not None:
        got = got - beta * previous[...]
    return got


def middle_body(*refs, alpha, beta):
    if beta is None:
        image_in, y_faces, x_low, x_high, current, matrix, values, *sums, work = refs
        previous = None
    else:
        image_in, y_faces, x_low, x_high, current, previous, matrix, values, *sums, work = refs
    work[...] = image_in[...]
    got = updated(work, y_faces, x_low, x_high, current, previous, alpha, beta)
    values[...] = got
    cell_product(got, matrix, *sums)


def block_places(count, half_rows):
    pairs = [(i, j) for i in range(count) for j in range(i, count)]
    size = -(-len(pairs) // 2)
    return {
        pair: n // size * half_rows + n % size * LANES for n, pair in enumerate(pairs)
    }


def half_correlation(which, values, out):
    width = values.shape[1]
    half_rows = out.shape[0]
    high = values.astype(jnp.bfloat16)
    low = (values - high.astype(jnp.float32)).astype(jnp.bfloat16)

    def product(a, b):
        return lax.dot_general(
            a, b, (((0,), (0,)), ((), ())), preferred_element_type=jnp.float32
        )

    strips = {}
    for (i, j), at in block_places(width // LANES, half_rows).items():
        if at // half_rows == which:
            strips.setdefault(i, []).append((j, at - which * half_rows))
    for i, found in strips.items():
        rows = slice(i * LANES, (i + 1) * LANES)
        cols = slice(found[0][0] * LANES, (found[-1][0] + 1) * LANES)
        strip = (
            product(high[:, rows], low[:, cols]) + product(low[:, rows], high[:, cols])
        ) + product(high[:, rows], high[:, cols])
        for n, (_, at) in enumerate(found):
            out[at : at + LANES] = strip[:, n * LANES : (n + 1) * LANES]


def chosen_half(number, values, out):
    for which in range(2):

        @pl.when(number == which)
        def _():
            half_correlation(which, values[...], out)


def last_body(
    mine, image_in, y_face, x_low, current, previous, stored, other, work, own, sem, *, alpha, beta
):
    edge = image_in.shape[0]
    width = image_in.shape[3]
    work[...] = image_in[...]
    got = updated(work, y_face, x_low, None, current, previous, alpha, beta)
    got = got[: edge - 1, : edge - 1]
    where = lax.broadcasted_iota(jnp.int32, got.shape, 2)
    got = jnp.where(where == edge - 1, 0.0, got)
    own[...] = got.reshape((edge - 1) ** 2 * edge, width)
    keep = pltpu.make_async_copy(own, stored, sem)
    keep.start()
    chosen_half(1 - mine[0], own, other)
    keep.wait()


def kept_body(mine, stored, half, own, sem):
    load = pltpu.make_async_copy(stored, own, sem)
    load.start()
    load.wait()
    chosen_half(mine[0], own, half)


def swap(block, axis, distance):
    count = lax.axis_size(axis)
    return lax.ppermute(block, axis, [(i, i ^ distance) for i in range(count)])


def stages_of(axis, size):
    stages, stride = [], 1
    while stride < size:
        radix = 2 if axis == "narrow" and stride == 1 else 4
        radix = min(radix, size // stride)
        stages.append((axis, stride, radix))
        stride *= radix
    return stages


def all_stages():
    return stages_of("narrow", lax.axis_size("narrow")) + stages_of(
        "wide", lax.axis_size("wide")
    )


def cut_rows(rows):
    cut = SUB
    for _, _, radix in all_stages()[:-1]:
        cut *= radix
    return -(-rows // cut) * cut


def cut_body(mine, *refs, count):
    terms, (*parts, work) = refs[:count], refs[count:]
    got = terms[0][...]
    for term in terms[1:]:
        got = got + term[...]
    work[...] = got
    rows = parts[0].shape[0]
    for d, part in enumerate(parts):
        part[...] = work[pl.ds(pl.multiple_of((mine[0] ^ d) * rows, SUB), rows)]


def digit(stage):
    axis, stride, radix = stage
    return (lax.axis_index(axis) // stride % radix).astype(jnp.int32)[None]


def summed(kept, other):
    lanes = kept.shape[1]
    stages = all_stages()
    parts = [kept, other]
    for stage, after in zip(stages[:-1], stages[1:]):
        axis, stride, _ = stage
        terms = [parts[0]] + [
            swap(part, axis, d * stride) for d, part in enumerate(parts[1:], 1)
        ]
        rows, radix = terms[0].shape[0], after[2]
        if after == stages[-1]:
            radix = 1
        parts = vmem_call(
            functools.partial(cut_body, count=len(terms)),
            (f32(rows // radix, lanes),) * radix,
            scratch=[pltpu.VMEM((rows, lanes), jnp.float32)],
            scalars=1,
        )(digit(after) if radix > 1 else jnp.zeros((1,), jnp.int32), *terms)
    block = parts[0]
    axis, stride, radix = stages[-1]
    got = [block] + [swap(block, axis, d * stride) for d in range(1, radix)]
    while len(got) > 1:
        got = [a + b for a, b in zip(got[::2], got[1::2])]
    block = got[0]
    for axis, stride, radix in reversed(stages[:-1]):
        mine = lax.axis_index(axis) // stride % radix
        parts = jnp.zeros((radix,) + block.shape, block.dtype)
        parts = lax.dynamic_update_index_in_dim(parts, block, mine, 0)
        for d in range(1, radix):
            parts = lax.dynamic_update_index_in_dim(
                parts, swap(block, axis, d * stride), mine ^ d, 0
            )
        block = parts.reshape(-1, lanes)
    return block


def lane_spread(tile, column):
    return jnp.broadcast_to(tile[:, column : column + 1], tile.shape)


def row_spread(tile, row):
    return jnp.broadcast_to(tile[row : row + 1, :], tile.shape)


def total(terms):
    while len(terms) > 1:
        terms = [a + b for a, b in zip(terms[::2], terms[1::2])]
    return terms[0]


def inverse_factor(block):
    size = block.shape[0]
    steps, per = size // SUB, SLAB // SUB
    tiles = [block[SUB * t : SUB * (t + 1)] for t in range(steps)]
    rows = lax.broadcasted_iota(jnp.int32, (SUB, size), 0)
    cols = lax.broadcasted_iota(jnp.int32, (SUB, size), 1)
    done = [None] * steps
    for s in range(0, steps, per):
        base = SUB * s
        own = (cols >= base) & (cols < base + SLAB)
        col = [
            {
                t: lane_spread(tiles[t], base + d)
                for t in range(s, s + per)
                if SUB * (t - s + 1) > d
            }
            for d in range(SLAB)
        ]
        before = list(tiles)
        for t in range(s, s + per):
            unit = jnp.where(cols == rows + SUB * t, 1.0, 0.0)
            tiles[t] = jnp.where(own, unit, tiles[t])
        for t in range(s + per, steps):
            tiles[t] = jnp.where(own, 0.0, tiles[t])

        def at(column, r):
            return row_spread(column[s + r // SUB], r % SUB)

        low, scale = [], []
        for k in range(0, SLAB, 2):
            x, y = col[k], col[k + 1]
            a, b, c = at(x, k), at(x, k + 1), at(y, k + 1)
            root = lax.rsqrt(a)
            next_root = lax.rsqrt(a * c - b * b)
            over = next_root * next_root
            p, q, u = {}, {}, {}
            for t in y:
                u[t] = a * y[t] - b * x[t]
                p[t] = (c * x[t] - b * y[t]) * over
                q[t] = u[t] * over
            for d in range(k + 2, SLAB):
                xd, yd = at(x, d), at(y, d)
                for t in col[d]:
                    col[d][t] = col[d][t] - (p[t] * xd + q[t] * yd)
            both = root * next_root
            here, r = s + k // SUB, k % SUB
            first = row_spread(tiles[here], r)
            second = row_spread(tiles[here], r + 1)
            for t in y:
                pm, qm = p[t], q[t]
                if t == here:
                    ratio = jnp.where(rows == r + 1, b * (root * root), 0.0)
                    pm = jnp.where(rows > r + 1, pm, ratio)
                    qm = jnp.where(rows > r + 1, qm, 0.0)
                tiles[t] = tiles[t] - (pm * first + qm * second)
            low.append({t: x[t] * root for t in y})
            low.append({t: u[t] * both for t in y})
            scale += [root, a * both]
        upper = []
        for i in range(per):
            t = s + i
            factors = scale[SUB * i]
            for k in range(1, SUB):
                factors = jnp.where(rows == k, scale[SUB * i + k], factors)
            tiles[t] = tiles[t] * factors
            done[t] = jnp.where(cols < base + SLAB, tiles[t], 0.0)
            upper += [row_spread(tiles[t], k) for k in range(SUB)]
        yield None
        if s + per < steps:
            solved = [None] * SLAB
            for k in reversed(range(SLAB)):
                row = upper[k]
                for m in reversed(range(k + 1, SLAB)):
                    row = row - at(low[k], m) * solved[m]
                solved[k] = row * scale[k]
            for t in range(s + per, steps):
                tiles[t] = tiles[t] - total(
                    [
                        lane_spread(before[t], base + k) * solved[k]
                        for k in reversed(range(SLAB))
                    ]
                )
    yield jnp.concatenate(done, axis=0)


def ortho_body(corr, own, out, blocks, rest, done, sent, sems, *, root_nodes):
    width = own.shape[1]
    count = width // LANES
    nodes = own.shape[0]
    part = nodes // PARTS

    def span(k):
        return pl.ds(LANES * k, LANES)

    work = []

    def factored(block):
        share = -(-len(work) // (LANES // SLAB - 1))
        for got in inverse_factor(block):
            if got is None:
                for task in [work.pop(0) for _ in range(min(share, len(work)))]:
                    task()
        while work:
            work.pop(0)()
        return got

    rows_of = block_places(count, corr.shape[0] // 2)
    place = {pair: n for n, pair in enumerate(rows_of)}

    on_diagonal = lax.broadcasted_iota(
        jnp.int32, (LANES, LANES), 0
    ) == lax.broadcasted_iota(jnp.int32, (LANES, LANES), 1)
    over_row, over_col = [], []
    for i in range(count):
        at = rows_of[i, i]
        kept = jnp.where(on_diagonal, corr[at : at + LANES], 0.0)
        over_row.append(lax.rsqrt(jnp.sum(kept, axis=1, keepdims=True)))
        over_col.append(lax.rsqrt(jnp.sum(kept, axis=0, keepdims=True)))

    def piece(i, j):
        at = rows_of[i, j]
        return corr[at : at + LANES] * over_row[i] * over_col[j]

    def set_up():
        for (i, j), n in place.items():
            if j > 0:
                blocks[n] = piece(i, j)
        for j in range(count):
            rest[:, span(j)] = own[:, span(j)] * (over_col[j] * root_nodes)

    def store(k):
        return pltpu.make_async_copy(sent.at[k], out.at[:, :, span(k)], sems.at[k])

    def finish(rows, k, block):
        done[rows, :] = block
        first, last = rows.start // SUB, rows.stop // SUB
        shaped = block.reshape(last - first, SUB, LANES)
        sent[k, first:last] = shaped[:, : SUB - 1]

    work.append(set_up)
    inverse = factored(piece(0, 0))
    for k in range(count - 1):
        near = exact_dot(inverse, blocks[place[k, k + 1]])
        diagonal = blocks[place[k + 1, k + 1]] - exact_dot(near, near, ((0,), (0,)))
        ups = {k + 1: near}

        def up_of(j, k=k, inverse=inverse, ups=ups):
            ups[j] = exact_dot(inverse, blocks[place[k, j]])

        def update(i, j, ups=ups):
            n = place[i, j]
            blocks[n] = blocks[n] - exact_dot(ups[i], ups[j], ((0,), (0,)))

        def solve(rows, k=k, inverse=inverse):
            finish(rows, k, exact_dot(rest[rows, span(k)], inverse, ((1,), (1,))))

        def subtract(rows, j, ups=ups):
            rest[rows, span(j)] = rest[rows, span(j)] - exact_dot(done[rows, :], ups[j])

        strips = [slice(r, r + part) for r in range(0, nodes, part)]
        later = range(k + 2, count)
        work += [functools.partial(up_of, j) for j in later]
        work += [
            functools.partial(update, i, j)
            for i in range(k + 1, count)
            for j in range(max(i, k + 2), count)
        ]
        work += [functools.partial(solve, rows) for rows in strips]
        work += [
            functools.partial(subtract, rows, j)
            for j in range(k + 1, count)
            for rows in strips
        ]
        inverse = factored(diagonal)
    last = count - 1
    finish(
        slice(0, nodes),
        last,
        exact_dot(rest[:, span(last)], inverse, ((1,), (1,))),
    )
    for k in range(count):
        store(k).start()
    for k in range(count):
        store(k).wait()


def to_next(block, axis, distance):
    count = lax.axis_size(axis)
    return lax.ppermute(block, axis, [(i, (i + distance) % count) for i in range(count)])


def from_next_both(block):
    rows, columns = lax.axis_size("wide"), lax.axis_size("narrow")
    route = [
        ((i + 1) % rows * columns + (j + 1) % columns, i * columns + j)
        for i in range(rows)
        for j in range(columns)
    ]
    return lax.ppermute(block, ("wide", "narrow"), route)


def y_exchange(sent):
    if lax.axis_size("narrow") == 2:
        return to_next(sent, "narrow", 1)
    return jnp.concatenate(
        [to_next(sent[:1], "narrow", 1), to_next(sent[1:], "narrow", -1)]
    )


def on_device(orbitals, cell_matrix, cell_order):
    order_now = orbitals.shape[0]
    edge = order_now + 1
    width = orbitals.shape[3]
    box = f32(edge, edge, edge, width)
    plane, sent = f32(edge, edge, width), f32(edge * order_now, width)
    sums = (box, plane, plane, f32(2, edge, edge, width))
    cell_nodes = edge**3
    (matrix,) = vmem_call(
        permute_body,
        (jax.ShapeDtypeStruct((cell_nodes, cell_nodes), jnp.bfloat16),),
        flops=4 * cell_nodes**3,
    )(
        cell_matrix.reshape(cell_nodes, cell_nodes),
        cell_order.reshape(cell_nodes, 1),
    )

    x_next = to_next(orbitals[:1], "wide", -1)
    corner = from_next_both(orbitals[:1, :1])
    y_next = to_next(orbitals[:, :1], "narrow", -1)
    product_flops = 2 * cell_nodes**2 * width
    current, image, x_first, x_last, y_sent = vmem_call(
        first_body, (box, *sums), flops=product_flops
    )(orbitals, x_next, y_next, corner, matrix)

    half_width = (band_high - band_low) / 2.0
    sigma_now = half_width / (anchor - (band_low + band_high) / 2.0)
    tau_value = 2.0 / sigma_now
    alpha, beta, previous = sigma_now / half_width, None, None
    for degree_step in range(1, DEG):
        y_faces = y_exchange(y_sent)
        x_last, x_first = vmem_call(edge_body, (sent, sent))(
            x_last, x_first, y_faces
        )
        x_high = to_next(x_first, "wide", -1)
        x_low = to_next(x_last, "wide", 1)
        operands = [image, y_faces, x_low, x_high, current]
        if previous is not None:
            operands.append(previous)
        next_values, image, x_first, x_last, y_sent = vmem_call(
            functools.partial(middle_body, alpha=alpha, beta=beta),
            (box, *sums),
            scratch=[pltpu.VMEM(box.shape, jnp.float32)],
            flops=product_flops,
        )(*operands, matrix)
        previous, current = current, next_values
        sigma_new = 1.0 / (tau_value - sigma_now)
        alpha, beta = 2.0 * sigma_new / half_width, sigma_now * sigma_new
        sigma_now = sigma_new

    y_low = to_next(y_sent[:1], "narrow", 1)
    (x_last,) = vmem_call(edge_body, (sent,))(x_last, y_low)
    x_low = to_next(x_last, "wide", 1)
    blocks = width // LANES
    rows = cut_rows(blocks * (blocks + 1) // 2 * LANES)
    first_stage = all_stages()[0]
    assert first_stage[2] == 2
    block_shape, half_shape = f32(order_now**2 * edge, width), f32(rows // 2, LANES)
    half_flops = 3 * cell_nodes * width**2
    stored, other = vmem_call(
        functools.partial(last_body, alpha=alpha, beta=beta),
        (block_shape, half_shape),
        scratch=[
            pltpu.VMEM(box.shape, jnp.float32),
            pltpu.VMEM(block_shape.shape, jnp.float32),
            pltpu.SemaphoreType.DMA,
        ],
        flops=half_flops,
        scalars=1,
        hbm_out=(0,),
    )(digit(first_stage), image, y_low, x_low, current, previous)
    (kept,) = vmem_call(
        kept_body,
        (half_shape,),
        scratch=[
            pltpu.VMEM(block_shape.shape, jnp.float32),
            pltpu.SemaphoreType.DMA,
        ],
        flops=half_flops,
        scalars=1,
        hbm_in=(1,),
    )(digit(first_stage), stored)

    nodes = order_now**3 * lax.axis_size("wide") * lax.axis_size("narrow")
    corr = summed(kept, other)
    (out,) = vmem_call(
        functools.partial(ortho_body, root_nodes=nodes**0.5),
        (f32(order_now**2, order_now, width),),
        scratch=[
            pltpu.VMEM((blocks * (blocks + 1) // 2, LANES, LANES), jnp.float32),
            pltpu.VMEM(block_shape.shape, jnp.float32),
            pltpu.VMEM((block_shape.shape[0], LANES), jnp.float32),
            pltpu.VMEM((blocks, order_now**2, order_now, LANES), jnp.float32),
            pltpu.SemaphoreType.DMA((blocks,)),
        ],
        flops=width**3,
        hbm_out=(0,),
    )(corr, stored)
    return out.reshape(orbitals.shape)


def solution(mesh):
    return jax.shard_map(
        on_device,
        mesh=mesh,
        in_specs=(
            P("wide", "narrow", None, None),
            P("wide", "narrow", None, None, None),
            P("wide", "narrow", None, None),
        ),
        out_specs=P("wide", "narrow", None, None),
        check_vma=False,
    )
```

```python
import functools

import jax
import jax.numpy as jnp
from jax import lax
from jax.experimental import pallas as pl
from jax.experimental.pallas import tpu as pltpu
from jax.sharding import PartitionSpec as P

DEG = 4
SUB = 8
LANES = 128
SLAB = 16
PARTS = 1
VMEM_LIMIT = 6 << 20


band_low = 4.0
band_high = 34.0
anchor = 0.0


def vmem_call(body, out_shapes, scratch=(), flops=0, scalars=0, hbm_in=(), hbm_out=()):
    def spec(in_hbm):
        return pl.BlockSpec(memory_space=pltpu.HBM if in_hbm else pltpu.VMEM)

    def call(*operands):
        operands = [
            x
            if n < scalars
            else pltpu.with_memory_space_constraint(
                x, pltpu.HBM if n in hbm_in else pltpu.VMEM
            )
            for n, x in enumerate(operands)
        ]
        outs = tuple(
            (pltpu.HBM if n in hbm_out else pltpu.VMEM)(x.shape, x.dtype)
            for n, x in enumerate(out_shapes)
        )
        return pl.pallas_call(
            body,
            out_shape=outs,
            in_specs=[pl.BlockSpec(memory_space=pltpu.SMEM)] * scalars
            + [spec(n in hbm_in) for n in range(scalars, len(operands))],
            out_specs=tuple(spec(n in hbm_out) for n in range(len(out_shapes))),
            scratch_shapes=list(scratch),
            compiler_params=pltpu.CompilerParams(vmem_limit_bytes=VMEM_LIMIT),
            cost_estimate=pl.CostEstimate(
                flops=flops, bytes_accessed=1 << 20, transcendentals=0
            ),
        )(*operands)

    return call


def f32(*shape):
    return jax.ShapeDtypeStruct(shape, jnp.float32)


def parts_of(x):
    high = x.astype(jnp.bfloat16)
    left = x - high.astype(jnp.float32)
    middle = left.astype(jnp.bfloat16)
    low = (left - middle.astype(jnp.float32)).astype(jnp.bfloat16)
    return high, middle, low


def exact_dot(a, b, dims=(1, 0)):
    (ah, am, al), (bh, bm, bl) = a, b
    return lax.dot_general(
        jnp.concatenate([ah, ah, am, am, ah, al], axis=dims[0]),
        jnp.concatenate([bh, bm, bh, bm, bl, bh], axis=dims[1]),
        (((dims[0],), (dims[1],)), ((), ())),
        preferred_element_type=jnp.float32,
    )


def permute_body(matrix, order, out):
    count = matrix.shape[0]
    pick = (
        lax.broadcasted_iota(jnp.int32, (count, count), 1) == order[...]
    ).astype(jnp.bfloat16)
    half = lax.dot_general(
        matrix[...],
        pick,
        (((1,), (0,)), ((), ())),
        preferred_element_type=jnp.float32,
    ).astype(jnp.bfloat16)
    out[...] = lax.dot_general(
        half, pick, (((0,), (0,)), ((), ())), preferred_element_type=jnp.float32
    ).astype(jnp.bfloat16)


def cell_product(values, matrix, image, x_first, x_last, y_sent):
    edge = values.shape[0]
    width = values.shape[3]
    rows = values.reshape(edge**3, width).astype(jnp.bfloat16)
    products = jnp.dot(matrix[...], rows, preferred_element_type=jnp.float32)
    products = products.reshape(edge, edge, edge, width)
    wrap = products[:, :, :1] + products[:, :, edge - 1 :]
    where = lax.broadcasted_iota(jnp.int32, products.shape, 2)
    products = jnp.where((where == 0) | (where == edge - 1), wrap, products)
    image[...] = products
    x_first[...] = products[0]
    x_last[...] = products[edge - 1]
    y_sent[0] = products[:, edge - 1]
    y_sent[1] = products[:, 0]


def first_body(own, x_next, y_next, corner, matrix, values, *sums):
    order_now = own.shape[0]
    values[:order_now, :order_now, :order_now] = own[...]
    values[order_now:, :order_now, :order_now] = x_next[...]
    values[:order_now, order_now:, :order_now] = y_next[...]
    values[order_now:, order_now:, :order_now] = corner[...]
    values[:, :, order_now:] = values[:, :, :1]
    cell_product(values[...], matrix, *sums)


def edge_body(*refs):
    *planes, y_faces = refs[: len(refs) // 2 + 1]
    outs = refs[len(refs) // 2 + 1 :]
    edge = planes[0].shape[0]
    order_now = edge - 1
    for plane, out, at in zip(planes, outs, (edge - 1, 0)):
        for b in range(edge):
            row = plane[b]
            if b == 0:
                row = row + y_faces[0, at]
            if b == edge - 1 and y_faces.shape[0] > 1:
                row = row + y_faces[1, at]
            out[order_now * b : order_now * (b + 1)] = row[:order_now]


def updated(image, y_faces, x_low, x_high, current, previous, alpha, beta):
    center = (band_low + band_high) / 2.0
    edge = image.shape[0]
    image[:, 0] = image[:, 0] + y_faces[0]
    if y_faces.shape[0] > 1:
        image[:, edge - 1] = image[:, edge - 1] + y_faces[1]
    order_now = edge - 1
    for at, got in ((0, x_low), (edge - 1, x_high)):
        if got is not None:
            for b in range(edge):
                first = order_now * b
                image[at, b, :order_now] += got[first : first + order_now]
                image[at, b, order_now:] += got[first : first + 1]
    got = (image[...] - center * current[...]) * alpha
    if previous is not None:
        got = got - beta * previous[...]
    return got


def middle_body(*refs, alpha, beta):
    if beta is None:
        image_in, y_faces, x_low, x_high, current, matrix, values, *sums, work = refs
        previous = None
    else:
        image_in, y_faces, x_low, x_high, current, previous, matrix, values, *sums, work = refs
    work[...] = image_in[...]
    got = updated(work, y_faces, x_low, x_high, current, previous, alpha, beta)
    values[...] = got
    cell_product(got, matrix, *sums)


def block_places(count, half_rows):
    pairs = [(i, j) for i in range(count) for j in range(i, count)]
    size = -(-len(pairs) // 2)
    return {
        pair: n // size * half_rows + n % size * LANES for n, pair in enumerate(pairs)
    }


def half_correlation(which, values, out):
    width = values.shape[1]
    half_rows = out.shape[0]
    high = values.astype(jnp.bfloat16)
    low = (values - high.astype(jnp.float32)).astype(jnp.bfloat16)

    def product(a, b):
        return lax.dot_general(
            a, b, (((0,), (0,)), ((), ())), preferred_element_type=jnp.float32
        )

    strips = {}
    for (i, j), at in block_places(width // LANES, half_rows).items():
        if at // half_rows == which:
            strips.setdefault(i, []).append((j, at - which * half_rows))
    for i, found in strips.items():
        rows = slice(i * LANES, (i + 1) * LANES)
        cols = slice(found[0][0] * LANES, (found[-1][0] + 1) * LANES)
        strip = (
            product(high[:, rows], low[:, cols]) + product(low[:, rows], high[:, cols])
        ) + product(high[:, rows], high[:, cols])
        for n, (_, at) in enumerate(found):
            out[at : at + LANES] = strip[:, n * LANES : (n + 1) * LANES]


def chosen_half(number, values, out):
    for which in range(2):

        @pl.when(number == which)
        def _():
            half_correlation(which, values[...], out)


def last_body(
    mine, image_in, y_face, x_low, current, previous, stored, other, work, own, sem, *, alpha, beta
):
    edge = image_in.shape[0]
    width = image_in.shape[3]
    work[...] = image_in[...]
    got = updated(work, y_face, x_low, None, current, previous, alpha, beta)
    got = got[: edge - 1, : edge - 1]
    where = lax.broadcasted_iota(jnp.int32, got.shape, 2)
    got = jnp.where(where == edge - 1, 0.0, got)
    own[...] = got.reshape((edge - 1) ** 2 * edge, width)
    keep = pltpu.make_async_copy(own, stored, sem)
    keep.start()
    chosen_half(1 - mine[0], own, other)
    keep.wait()


def kept_body(mine, stored, half, own, sem):
    load = pltpu.make_async_copy(stored, own, sem)
    load.start()
    load.wait()
    chosen_half(mine[0], own, half)


def swap(block, axis, distance):
    count = lax.axis_size(axis)
    return lax.ppermute(block, axis, [(i, i ^ distance) for i in range(count)])


def stages_of(axis, size):
    stages, stride = [], 1
    while stride < size:
        radix = 2 if axis == "narrow" and stride == 1 else 4
        radix = min(radix, size // stride)
        stages.append((axis, stride, radix))
        stride *= radix
    return stages


def all_stages():
    return stages_of("narrow", lax.axis_size("narrow")) + stages_of(
        "wide", lax.axis_size("wide")
    )


def cut_rows(rows):
    cut = SUB
    for _, _, radix in all_stages()[:-1]:
        cut *= radix
    return -(-rows // cut) * cut


def cut_body(mine, *refs, count):
    terms, (*parts, work) = refs[:count], refs[count:]
    got = terms[0][...]
    for term in terms[1:]:
        got = got + term[...]
    work[...] = got
    rows = parts[0].shape[0]
    for d, part in enumerate(parts):
        part[...] = work[pl.ds(pl.multiple_of((mine[0] ^ d) * rows, SUB), rows)]


def digit(stage):
    axis, stride, radix = stage
    return (lax.axis_index(axis) // stride % radix).astype(jnp.int32)[None]


def summed(kept, other):
    lanes = kept.shape[1]
    stages = all_stages()
    parts = [kept, other]
    for stage, after in zip(stages[:-1], stages[1:]):
        axis, stride, _ = stage
        terms = [parts[0]] + [
            swap(parts[d], axis, d * stride) for d in reversed(range(1, len(parts)))
        ]
        rows, radix = terms[0].shape[0], after[2]
        if after == stages[-1]:
            radix = 1
        parts = vmem_call(
            functools.partial(cut_body, count=len(terms)),
            (f32(rows // radix, lanes),) * radix,
            scratch=[pltpu.VMEM((rows, lanes), jnp.float32)],
            scalars=1,
        )(digit(after) if radix > 1 else jnp.zeros((1,), jnp.int32), *terms)
    block = parts[0]
    axis, stride, radix = stages[-1]
    got = [swap(block, axis, d * stride) for d in reversed(range(1, radix))]
    got = [block] + got[::-1]
    while len(got) > 1:
        got = [a + b for a, b in zip(got[::2], got[1::2])]
    block = got[0]
    for axis, stride, radix in reversed(stages[:-1]):
        mine = lax.axis_index(axis) // stride % radix
        parts = jnp.zeros((radix,) + block.shape, block.dtype)
        parts = lax.dynamic_update_index_in_dim(parts, block, mine, 0)
        for d in reversed(range(1, radix)):
            parts = lax.dynamic_update_index_in_dim(
                parts, swap(block, axis, d * stride), mine ^ d, 0
            )
        block = parts.reshape(-1, lanes)
    return block


def lane_spread(tile, column):
    return jnp.broadcast_to(tile[:, column : column + 1], tile.shape)


def row_spread(tile, row):
    return jnp.broadcast_to(tile[row : row + 1, :], tile.shape)


def total(terms):
    while len(terms) > 1:
        terms = [a + b for a, b in zip(terms[::2], terms[1::2])]
    return terms[0]


def inverse_factor(block):
    size = block.shape[0]
    steps, per = size // SUB, SLAB // SUB
    tiles = [block[SUB * t : SUB * (t + 1)] for t in range(steps)]
    rows = lax.broadcasted_iota(jnp.int32, (SUB, size), 0)
    cols = lax.broadcasted_iota(jnp.int32, (SUB, size), 1)
    done = [None] * steps
    for s in range(0, steps, per):
        base = SUB * s
        own = (cols >= base) & (cols < base + SLAB)
        col = [
            {
                t: lane_spread(tiles[t], base + d)
                for t in range(s, s + per)
                if SUB * (t - s + 1) > d
            }
            for d in range(SLAB)
        ]
        before = list(tiles)
        for t in range(s, s + per):
            unit = jnp.where(cols == rows + SUB * t, 1.0, 0.0)
            tiles[t] = jnp.where(own, unit, tiles[t])
        for t in range(s + per, steps):
            tiles[t] = jnp.where(own, 0.0, tiles[t])

        def at(column, r):
            return row_spread(column[s + r // SUB], r % SUB)

        low, scale = [], []
        for k in range(0, SLAB, 2):
            x, y = col[k], col[k + 1]
            a, b, c = at(x, k), at(x, k + 1), at(y, k + 1)
            root = lax.rsqrt(a)
            next_root = lax.rsqrt(a * c - b * b)
            over = next_root * next_root
            p, q, u = {}, {}, {}
            for t in y:
                u[t] = a * y[t] - b * x[t]
                p[t] = (c * x[t] - b * y[t]) * over
                q[t] = u[t] * over
            for d in range(k + 2, SLAB):
                xd, yd = at(x, d), at(y, d)
                for t in col[d]:
                    col[d][t] = col[d][t] - (p[t] * xd + q[t] * yd)
            both = root * next_root
            here, r = s + k // SUB, k % SUB
            first = row_spread(tiles[here], r)
            second = row_spread(tiles[here], r + 1)
            for t in y:
                pm, qm = p[t], q[t]
                if t == here:
                    ratio = jnp.where(rows == r + 1, b * (root * root), 0.0)
                    pm = jnp.where(rows > r + 1, pm, ratio)
                    qm = jnp.where(rows > r + 1, qm, 0.0)
                tiles[t] = tiles[t] - (pm * first + qm * second)
            low.append({t: x[t] * root for t in y})
            low.append({t: u[t] * both for t in y})
            scale += [root, a * both]
        upper = []
        for i in range(per):
            t = s + i
            factors = scale[SUB * i]
            for k in range(1, SUB):
                factors = jnp.where(rows == k, scale[SUB * i + k], factors)
            tiles[t] = tiles[t] * factors
            done[t] = jnp.where(cols < base + SLAB, tiles[t], 0.0)
            upper += [row_spread(tiles[t], k) for k in range(SUB)]
        yield None
        if s + per < steps:
            solved = [None] * SLAB
            for k in reversed(range(SLAB)):
                row = upper[k]
                for m in reversed(range(k + 1, SLAB)):
                    row = row - at(low[k], m) * solved[m]
                solved[k] = row * scale[k]
            for t in range(s + per, steps):
                tiles[t] = tiles[t] - total(
                    [
                        lane_spread(before[t], base + k) * solved[k]
                        for k in reversed(range(SLAB))
                    ]
                )
    yield jnp.concatenate(done, axis=0)


def ortho_body(corr, own, out, blocks, rest, done, sent, sems, *, root_nodes):
    width = own.shape[1]
    count = width // LANES
    nodes = own.shape[0]
    part = nodes // PARTS

    def span(k):
        return pl.ds(LANES * k, LANES)

    work = []

    def factored(block):
        share = -(-len(work) // (LANES // SLAB - 1))
        for got in inverse_factor(block):
            if got is None:
                for task in [work.pop(0) for _ in range(min(share, len(work)))]:
                    task()
        while work:
            work.pop(0)()
        return got

    rows_of = block_places(count, corr.shape[0] // 2)
    place = {pair: n for n, pair in enumerate(rows_of)}

    on_diagonal = lax.broadcasted_iota(
        jnp.int32, (LANES, LANES), 0
    ) == lax.broadcasted_iota(jnp.int32, (LANES, LANES), 1)
    over_row, over_col = [], []
    for i in range(count):
        at = rows_of[i, i]
        kept = jnp.where(on_diagonal, corr[at : at + LANES], 0.0)
        over_row.append(lax.rsqrt(jnp.sum(kept, axis=1, keepdims=True)))
        over_col.append(lax.rsqrt(jnp.sum(kept, axis=0, keepdims=True)))

    def piece(i, j):
        at = rows_of[i, j]
        return corr[at : at + LANES] * over_row[i] * over_col[j]

    def set_up():
        for (i, j), n in place.items():
            if j > 0:
                blocks[n] = piece(i, j)
        for j in range(count):
            rest[:, span(j)] = own[:, span(j)] * (over_col[j] * root_nodes)

    def store(k):
        return pltpu.make_async_copy(sent.at[k], out.at[:, :, span(k)], sems.at[k])

    def finish(rows, k, block):
        done[rows, :] = block
        first, last = rows.start // SUB, rows.stop // SUB
        shaped = block.reshape(last - first, SUB, LANES)
        sent[k, first:last] = shaped[:, : SUB - 1]

    work.append(set_up)
    inverse = factored(piece(0, 0))
    for k in range(count - 1):
        inverse = parts_of(inverse)
        near = parts_of(exact_dot(inverse, parts_of(blocks[place[k, k + 1]])))
        diagonal = blocks[place[k + 1, k + 1]] - exact_dot(near, near, (0, 0))
        ups = {k + 1: near}

        def up_of(j, k=k, inverse=inverse, ups=ups):
            ups[j] = parts_of(exact_dot(inverse, parts_of(blocks[place[k, j]])))

        def update(i, j, ups=ups):
            n = place[i, j]
            blocks[n] = blocks[n] - exact_dot(ups[i], ups[j], (0, 0))

        def solve(rows, k=k, inverse=inverse):
            finish(rows, k, exact_dot(parts_of(rest[rows, span(k)]), inverse, (1, 1)))

        def subtract(rows, j, ups=ups):
            step = exact_dot(parts_of(done[rows, :]), ups[j])
            rest[rows, span(j)] = rest[rows, span(j)] - step

        strips = [slice(r, r + part) for r in range(0, nodes, part)]
        later = range(k + 2, count)
        work += [functools.partial(up_of, j) for j in later]
        work += [
            functools.partial(update, i, j)
            for i in range(k + 1, count)
            for j in range(max(i, k + 2), count)
        ]
        work += [functools.partial(solve, rows) for rows in strips]
        work += [
            functools.partial(subtract, rows, j)
            for j in range(k + 1, count)
            for rows in strips
        ]
        ahead = []
        if k + 2 == count:
            work.append(lambda: ahead.append(parts_of(rest[:, span(count - 1)])))
        inverse = factored(diagonal)
    last = count - 1
    finish(slice(0, nodes), last, exact_dot(ahead[0], parts_of(inverse), (1, 1)))
    for k in range(count):
        store(k).start()
    for k in range(count):
        store(k).wait()


def to_next(block, axis, distance):
    count = lax.axis_size(axis)
    return lax.ppermute(block, axis, [(i, (i + distance) % count) for i in range(count)])


def from_next_both(block):
    rows, columns = lax.axis_size("wide"), lax.axis_size("narrow")
    route = [
        ((i + 1) % rows * columns + (j + 1) % columns, i * columns + j)
        for i in range(rows)
        for j in range(columns)
    ]
    return lax.ppermute(block, ("wide", "narrow"), route)


def y_exchange(sent):
    if lax.axis_size("narrow") == 2:
        return to_next(sent, "narrow", 1)
    return jnp.concatenate(
        [to_next(sent[:1], "narrow", 1), to_next(sent[1:], "narrow", -1)]
    )


def on_device(orbitals, cell_matrix, cell_order):
    order_now = orbitals.shape[0]
    edge = order_now + 1
    width = orbitals.shape[3]
    box = f32(edge, edge, edge, width)
    plane, sent = f32(edge, edge, width), f32(edge * order_now, width)
    sums = (box, plane, plane, f32(2, edge, edge, width))
    cell_nodes = edge**3
    (matrix,) = vmem_call(
        permute_body,
        (jax.ShapeDtypeStruct((cell_nodes, cell_nodes), jnp.bfloat16),),
        flops=4 * cell_nodes**3,
    )(
        cell_matrix.reshape(cell_nodes, cell_nodes),
        cell_order.reshape(cell_nodes, 1),
    )

    x_next = to_next(orbitals[:1], "wide", -1)
    corner = from_next_both(orbitals[:1, :1])
    y_next = to_next(orbitals[:, :1], "narrow", -1)
    product_flops = 2 * cell_nodes**2 * width
    current, image, x_first, x_last, y_sent = vmem_call(
        first_body, (box, *sums), flops=product_flops
    )(orbitals, x_next, y_next, corner, matrix)

    half_width = (band_high - band_low) / 2.0
    sigma_now = half_width / (anchor - (band_low + band_high) / 2.0)
    tau_value = 2.0 / sigma_now
    alpha, beta, previous = sigma_now / half_width, None, None
    for degree_step in range(1, DEG):
        y_faces = y_exchange(y_sent)
        x_last, x_first = vmem_call(edge_body, (sent, sent))(
            x_last, x_first, y_faces
        )
        x_high = to_next(x_first, "wide", -1)
        x_low = to_next(x_last, "wide", 1)
        operands = [image, y_faces, x_low, x_high, current]
        if previous is not None:
            operands.append(previous)
        next_values, image, x_first, x_last, y_sent = vmem_call(
            functools.partial(middle_body, alpha=alpha, beta=beta),
            (box, *sums),
            scratch=[pltpu.VMEM(box.shape, jnp.float32)],
            flops=product_flops,
        )(*operands, matrix)
        previous, current = current, next_values
        sigma_new = 1.0 / (tau_value - sigma_now)
        alpha, beta = 2.0 * sigma_new / half_width, sigma_now * sigma_new
        sigma_now = sigma_new

    y_low = to_next(y_sent[:1], "narrow", 1)
    (x_last,) = vmem_call(edge_body, (sent,))(x_last, y_low)
    x_low = to_next(x_last, "wide", 1)
    blocks = width // LANES
    rows = cut_rows(blocks * (blocks + 1) // 2 * LANES)
    first_stage = all_stages()[0]
    assert first_stage[2] == 2
    block_shape, half_shape = f32(order_now**2 * edge, width), f32(rows // 2, LANES)
    half_flops = 3 * cell_nodes * width**2
    stored, other = vmem_call(
        functools.partial(last_body, alpha=alpha, beta=beta),
        (block_shape, half_shape),
        scratch=[
            pltpu.VMEM(box.shape, jnp.float32),
            pltpu.VMEM(block_shape.shape, jnp.float32),
            pltpu.SemaphoreType.DMA,
        ],
        flops=half_flops,
        scalars=1,
        hbm_out=(0,),
    )(digit(first_stage), image, y_low, x_low, current, previous)
    (kept,) = vmem_call(
        kept_body,
        (half_shape,),
        scratch=[
            pltpu.VMEM(block_shape.shape, jnp.float32),
            pltpu.SemaphoreType.DMA,
        ],
        flops=half_flops,
        scalars=1,
        hbm_in=(1,),
    )(digit(first_stage), stored)

    nodes = order_now**3 * lax.axis_size("wide") * lax.axis_size("narrow")
    corr = summed(kept, other)
    (out,) = vmem_call(
        functools.partial(ortho_body, root_nodes=nodes**0.5),
        (f32(order_now**2, order_now, width),),
        scratch=[
            pltpu.VMEM((blocks * (blocks + 1) // 2, LANES, LANES), jnp.float32),
            pltpu.VMEM(block_shape.shape, jnp.float32),
            pltpu.VMEM((block_shape.shape[0], LANES), jnp.float32),
            pltpu.VMEM((blocks, order_now**2, order_now, LANES), jnp.float32),
            pltpu.SemaphoreType.DMA((blocks,)),
        ],
        flops=width**3,
        hbm_out=(0,),
    )(corr, stored)
    return out.reshape(orbitals.shape)


def solution(mesh):
    return jax.shard_map(
        on_device,
        mesh=mesh,
        in_specs=(
            P("wide", "narrow", None, None),
            P("wide", "narrow", None, None, None),
            P("wide", "narrow", None, None),
        ),
        out_specs=P("wide", "narrow", None, None),
        check_vma=False,
    )
```

```python
import functools

import jax
import jax.numpy as jnp
from jax import lax
from jax.experimental import pallas as pl
from jax.experimental.pallas import tpu as pltpu
from jax.sharding import PartitionSpec as P

DEG = 4
SUB = 8
LANES = 128
SLAB = 16
PARTS = 1
VMEM_LIMIT = 6 << 20


band_low = 4.0
band_high = 34.0
anchor = 0.0


def vmem_call(body, out_shapes, scratch=(), flops=0, scalars=0, hbm_in=(), hbm_out=()):
    def spec(in_hbm):
        return pl.BlockSpec(memory_space=pltpu.HBM if in_hbm else pltpu.VMEM)

    def call(*operands):
        operands = [
            x
            if n < scalars
            else pltpu.with_memory_space_constraint(
                x, pltpu.HBM if n in hbm_in else pltpu.VMEM
            )
            for n, x in enumerate(operands)
        ]
        outs = tuple(
            (pltpu.HBM if n in hbm_out else pltpu.VMEM)(x.shape, x.dtype)
            for n, x in enumerate(out_shapes)
        )
        return pl.pallas_call(
            body,
            out_shape=outs,
            in_specs=[pl.BlockSpec(memory_space=pltpu.SMEM)] * scalars
            + [spec(n in hbm_in) for n in range(scalars, len(operands))],
            out_specs=tuple(spec(n in hbm_out) for n in range(len(out_shapes))),
            scratch_shapes=list(scratch),
            compiler_params=pltpu.CompilerParams(vmem_limit_bytes=VMEM_LIMIT),
            cost_estimate=pl.CostEstimate(
                flops=flops, bytes_accessed=1 << 20, transcendentals=0
            ),
        )(*operands)

    return call


def f32(*shape):
    return jax.ShapeDtypeStruct(shape, jnp.float32)


def parts_of(x):
    high = x.astype(jnp.bfloat16)
    left = x - high.astype(jnp.float32)
    middle = left.astype(jnp.bfloat16)
    low = (left - middle.astype(jnp.float32)).astype(jnp.bfloat16)
    return high, middle, low


def exact_dot(a, b, dims=(1, 0)):
    (ah, am, al), (bh, bm, bl) = a, b
    return lax.dot_general(
        jnp.concatenate([ah, ah, am, am, ah, al], axis=dims[0]),
        jnp.concatenate([bh, bm, bh, bm, bl, bh], axis=dims[1]),
        (((dims[0],), (dims[1],)), ((), ())),
        preferred_element_type=jnp.float32,
    )


def permute_body(matrix, order, out):
    count = matrix.shape[0]
    pick = (
        lax.broadcasted_iota(jnp.int32, (count, count), 1) == order[...]
    ).astype(jnp.bfloat16)
    half = lax.dot_general(
        matrix[...],
        pick,
        (((1,), (0,)), ((), ())),
        preferred_element_type=jnp.float32,
    ).astype(jnp.bfloat16)
    out[...] = lax.dot_general(
        half, pick, (((0,), (0,)), ((), ())), preferred_element_type=jnp.float32
    ).astype(jnp.bfloat16)


def cell_product(values, matrix, image, *planes):
    edge = values.shape[0]
    width = values.shape[3]
    rows = values.reshape(edge**3, width).astype(jnp.bfloat16)
    products = jnp.dot(matrix[...], rows, preferred_element_type=jnp.float32)
    products = products.reshape(edge, edge, edge, width)
    wrap = products[:, :, :1] + products[:, :, edge - 1 :]
    where = lax.broadcasted_iota(jnp.int32, products.shape, 2)
    products = jnp.where((where == 0) | (where == edge - 1), wrap, products)
    image[...] = products
    x_last, *x_first, y_sent = planes
    x_last[...] = products[edge - 1]
    y_sent[0] = products[:, edge - 1]
    if x_first:
        x_first[0][...] = products[0]
        y_sent[1] = products[:, 0]


def first_body(own, x_next, y_next, matrix, values, *sums):
    order_now = own.shape[0]
    values[:order_now, :order_now, :order_now] = own[...]
    values[order_now:, :order_now, :order_now] = x_next[...]
    values[:, order_now:, :order_now] = y_next[...]
    values[:, :, order_now:] = values[:, :, :1]
    cell_product(values[...], matrix, *sums)


def edge_body(plane, y_faces, *refs, at):
    out = refs[-1]
    edge = plane.shape[0]
    order_now = edge - 1
    for b in range(edge):
        row = plane[b]
        if b == 0:
            row = row + y_faces[0, at]
        if b == edge - 1 and y_faces.shape[0] > 1:
            row = row + y_faces[1, at]
        out[order_now * b : order_now * (b + 1)] = row[:order_now]


def updated(image, y_faces, x_low, x_high, current, previous, alpha, beta):
    center = (band_low + band_high) / 2.0
    edge = image.shape[0]
    image[:, 0] = image[:, 0] + y_faces[0]
    if y_faces.shape[0] > 1:
        image[:, edge - 1] = image[:, edge - 1] + y_faces[1]
    order_now = edge - 1
    for at, got in ((0, x_low), (edge - 1, x_high)):
        if got is not None:
            for b in range(edge):
                first = order_now * b
                image[at, b, :order_now] += got[first : first + order_now]
                image[at, b, order_now:] += got[first : first + 1]
    got = (image[...] - center * current[...]) * alpha
    if previous is not None:
        got = got - beta * previous[...]
    return got


def middle_body(*refs, alpha, beta):
    if beta is None:
        image_in, y_faces, x_low, x_high, current, matrix, values, *sums, work = refs
        previous = None
    else:
        image_in, y_faces, x_low, x_high, current, previous, matrix, values, *sums, work = refs
    work[...] = image_in[...]
    got = updated(work, y_faces, x_low, x_high, current, previous, alpha, beta)
    values[...] = got
    cell_product(got, matrix, *sums)


def block_places(count, half_rows):
    pairs = [(i, j) for i in range(count) for j in range(i, count)]
    size = -(-len(pairs) // 2)
    return {
        pair: n // size * half_rows + n % size * LANES for n, pair in enumerate(pairs)
    }


def half_correlation(which, values, out):
    width = values.shape[1]
    half_rows = out.shape[0]
    high = values.astype(jnp.bfloat16)
    low = (values - high.astype(jnp.float32)).astype(jnp.bfloat16)

    def product(a, b):
        return lax.dot_general(
            a, b, (((0,), (0,)), ((), ())), preferred_element_type=jnp.float32
        )

    strips = {}
    for (i, j), at in block_places(width // LANES, half_rows).items():
        if at // half_rows == which:
            strips.setdefault(i, []).append((j, at - which * half_rows))
    for i, found in strips.items():
        rows = slice(i * LANES, (i + 1) * LANES)
        cols = slice(found[0][0] * LANES, (found[-1][0] + 1) * LANES)
        strip = (
            product(high[:, rows], low[:, cols]) + product(low[:, rows], high[:, cols])
        ) + product(high[:, rows], high[:, cols])
        for n, (_, at) in enumerate(found):
            out[at : at + LANES] = strip[:, n * LANES : (n + 1) * LANES]


def chosen_half(number, values, out):
    for which in range(2):

        @pl.when(number == which)
        def _():
            half_correlation(which, values[...], out)


def last_body(
    mine, image_in, y_face, x_low, current, previous, stored, other, work, own, sem, *, alpha, beta
):
    edge = image_in.shape[0]
    width = image_in.shape[3]
    work[...] = image_in[...]
    got = updated(work, y_face, x_low, None, current, previous, alpha, beta)
    got = got[: edge - 1, : edge - 1]
    where = lax.broadcasted_iota(jnp.int32, got.shape, 2)
    got = jnp.where(where == edge - 1, 0.0, got)
    own[...] = got.reshape((edge - 1) ** 2 * edge, width)
    keep = pltpu.make_async_copy(own, stored, sem)
    keep.start()
    chosen_half(1 - mine[0], own, other)
    keep.wait()


def kept_body(mine, stored, half, own, sem):
    load = pltpu.make_async_copy(stored, own, sem)
    load.start()
    load.wait()
    chosen_half(mine[0], own, half)


def swap(block, axis, distance):
    count = lax.axis_size(axis)
    return lax.ppermute(block, axis, [(i, i ^ distance) for i in range(count)])


def stages_of(axis, size):
    stages, stride = [], 1
    while stride < size:
        radix = 2 if axis == "narrow" and stride == 1 else 4
        radix = min(radix, size // stride)
        stages.append((axis, stride, radix))
        stride *= radix
    return stages


def all_stages():
    return stages_of("narrow", lax.axis_size("narrow")) + stages_of(
        "wide", lax.axis_size("wide")
    )


def cut_rows(rows):
    cut = SUB
    for _, _, radix in all_stages()[:-1]:
        cut *= radix
    return -(-rows // cut) * cut


def cut_body(mine, *refs, count):
    terms, (*parts, work) = refs[:count], refs[count:]
    got = terms[0][...]
    for term in terms[1:]:
        got = got + term[...]
    work[...] = got
    rows = parts[0].shape[0]
    for d, part in enumerate(parts):
        part[...] = work[pl.ds(pl.multiple_of((mine[0] ^ d) * rows, SUB), rows)]


def digit(stage):
    axis, stride, radix = stage
    return (lax.axis_index(axis) // stride % radix).astype(jnp.int32)[None]


def summed(kept, other):
    lanes = kept.shape[1]
    stages = all_stages()
    parts = [kept, other]
    for stage, after in zip(stages[:-1], stages[1:]):
        axis, stride, _ = stage
        terms = [parts[0]] + [
            swap(parts[d], axis, d * stride) for d in reversed(range(1, len(parts)))
        ]
        rows, radix = terms[0].shape[0], after[2]
        if after == stages[-1]:
            radix = 1
        parts = vmem_call(
            functools.partial(cut_body, count=len(terms)),
            (f32(rows // radix, lanes),) * radix,
            scratch=[pltpu.VMEM((rows, lanes), jnp.float32)],
            scalars=1,
        )(digit(after) if radix > 1 else jnp.zeros((1,), jnp.int32), *terms)
    block = parts[0]
    axis, stride, radix = stages[-1]
    got = [swap(block, axis, d * stride) for d in reversed(range(1, radix))]
    got = [block] + got[::-1]
    while len(got) > 1:
        got = [a + b for a, b in zip(got[::2], got[1::2])]
    block = got[0]
    for axis, stride, radix in reversed(stages[:-1]):
        mine = lax.axis_index(axis) // stride % radix
        parts = jnp.zeros((radix,) + block.shape, block.dtype)
        parts = lax.dynamic_update_index_in_dim(parts, block, mine, 0)
        for d in reversed(range(1, radix)):
            parts = lax.dynamic_update_index_in_dim(
                parts, swap(block, axis, d * stride), mine ^ d, 0
            )
        block = parts.reshape(-1, lanes)
    return block


def lane_spread(tile, column):
    return jnp.broadcast_to(tile[:, column : column + 1], tile.shape)


def row_spread(tile, row):
    return jnp.broadcast_to(tile[row : row + 1, :], tile.shape)


def total(terms):
    while len(terms) > 1:
        terms = [a + b for a, b in zip(terms[::2], terms[1::2])]
    return terms[0]


def inverse_factor(block):
    size = block.shape[0]
    steps, per = size // SUB, SLAB // SUB
    tiles = [block[SUB * t : SUB * (t + 1)] for t in range(steps)]
    rows = lax.broadcasted_iota(jnp.int32, (SUB, size), 0)
    cols = lax.broadcasted_iota(jnp.int32, (SUB, size), 1)
    done = [None] * steps
    for s in range(0, steps, per):
        base = SUB * s
        own = (cols >= base) & (cols < base + SLAB)
        col = [
            {
                t: lane_spread(tiles[t], base + d)
                for t in range(s, s + per)
                if SUB * (t - s + 1) > d
            }
            for d in range(SLAB)
        ]
        before = list(tiles)
        for t in range(s, s + per):
            unit = jnp.where(cols == rows + SUB * t, 1.0, 0.0)
            tiles[t] = jnp.where(own, unit, tiles[t])
        for t in range(s + per, steps):
            tiles[t] = jnp.where(own, 0.0, tiles[t])

        def at(column, r):
            return row_spread(column[s + r // SUB], r % SUB)

        low, scale = [], []
        for k in range(0, SLAB, 2):
            x, y = col[k], col[k + 1]
            a, b, c = at(x, k), at(x, k + 1), at(y, k + 1)
            root = lax.rsqrt(a)
            next_root = lax.rsqrt(a * c - b * b)
            over = next_root * next_root
            p, q, u = {}, {}, {}
            for t in y:
                u[t] = a * y[t] - b * x[t]
                p[t] = (c * x[t] - b * y[t]) * over
                q[t] = u[t] * over
            for d in range(k + 2, SLAB):
                xd, yd = at(x, d), at(y, d)
                for t in col[d]:
                    col[d][t] = col[d][t] - (p[t] * xd + q[t] * yd)
            both = root * next_root
            here, r = s + k // SUB, k % SUB
            first = row_spread(tiles[here], r)
            second = row_spread(tiles[here], r + 1)
            for t in y:
                pm, qm = p[t], q[t]
                if t == here:
                    ratio = jnp.where(rows == r + 1, b * (root * root), 0.0)
                    pm = jnp.where(rows > r + 1, pm, ratio)
                    qm = jnp.where(rows > r + 1, qm, 0.0)
                tiles[t] = tiles[t] - (pm * first + qm * second)
            low.append({t: x[t] * root for t in y})
            low.append({t: u[t] * both for t in y})
            scale += [root, a * both]
        upper = []
        for i in range(per):
            t = s + i
            factors = scale[SUB * i]
            for k in range(1, SUB):
                factors = jnp.where(rows == k, scale[SUB * i + k], factors)
            tiles[t] = tiles[t] * factors
            done[t] = jnp.where(cols < base + SLAB, tiles[t], 0.0)
            upper += [row_spread(tiles[t], k) for k in range(SUB)]
        yield None
        if s + per < steps:
            solved = [None] * SLAB
            for k in reversed(range(SLAB)):
                row = upper[k]
                for m in reversed(range(k + 1, SLAB)):
                    row = row - at(low[k], m) * solved[m]
                solved[k] = row * scale[k]
            for t in range(s + per, steps):
                tiles[t] = tiles[t] - total(
                    [
                        lane_spread(before[t], base + k) * solved[k]
                        for k in reversed(range(SLAB))
                    ]
                )
    yield jnp.concatenate(done, axis=0)


def ortho_body(corr, own, out, blocks, rest, done, sent, sems, *, root_nodes):
    width = own.shape[1]
    count = width // LANES
    nodes = own.shape[0]
    part = nodes // PARTS

    def span(k):
        return pl.ds(LANES * k, LANES)

    work = []

    def factored(block):
        share = -(-len(work) // (LANES // SLAB - 1))
        for got in inverse_factor(block):
            if got is None:
                for task in [work.pop(0) for _ in range(min(share, len(work)))]:
                    task()
        while work:
            work.pop(0)()
        return got

    rows_of = block_places(count, corr.shape[0] // 2)
    place = {pair: n for n, pair in enumerate(rows_of)}

    on_diagonal = lax.broadcasted_iota(
        jnp.int32, (LANES, LANES), 0
    ) == lax.broadcasted_iota(jnp.int32, (LANES, LANES), 1)
    over_row, over_col = [], []
    for i in range(count):
        at = rows_of[i, i]
        kept = jnp.where(on_diagonal, corr[at : at + LANES], 0.0)
        over_row.append(lax.rsqrt(jnp.sum(kept, axis=1, keepdims=True)))
        over_col.append(lax.rsqrt(jnp.sum(kept, axis=0, keepdims=True)))

    def piece(i, j):
        at = rows_of[i, j]
        return corr[at : at + LANES] * over_row[i] * over_col[j]

    def set_up():
        for (i, j), n in place.items():
            if j > 0:
                blocks[n] = piece(i, j)
        for j in range(count):
            rest[:, span(j)] = own[:, span(j)] * (over_col[j] * root_nodes)

    def store(k):
        return pltpu.make_async_copy(sent.at[k], out.at[:, :, span(k)], sems.at[k])

    def finish(rows, k, block):
        done[rows, :] = block
        first, last = rows.start // SUB, rows.stop // SUB
        shaped = block.reshape(last - first, SUB, LANES)
        sent[k, first:last] = shaped[:, : SUB - 1]

    work.append(set_up)
    inverse = factored(piece(0, 0))
    for k in range(count - 1):
        inverse = parts_of(inverse)
        near = parts_of(exact_dot(inverse, parts_of(blocks[place[k, k + 1]])))
        diagonal = blocks[place[k + 1, k + 1]] - exact_dot(near, near, (0, 0))
        ups = {k + 1: near}

        def up_of(j, k=k, inverse=inverse, ups=ups):
            ups[j] = parts_of(exact_dot(inverse, parts_of(blocks[place[k, j]])))

        def update(i, j, ups=ups):
            n = place[i, j]
            blocks[n] = blocks[n] - exact_dot(ups[i], ups[j], (0, 0))

        def solve(rows, k=k, inverse=inverse):
            finish(rows, k, exact_dot(parts_of(rest[rows, span(k)]), inverse, (1, 1)))

        def subtract(rows, j, ups=ups):
            step = exact_dot(parts_of(done[rows, :]), ups[j])
            rest[rows, span(j)] = rest[rows, span(j)] - step

        strips = [slice(r, r + part) for r in range(0, nodes, part)]
        later = range(k + 2, count)
        work += [functools.partial(up_of, j) for j in later]
        work += [
            functools.partial(update, i, j)
            for i in range(k + 1, count)
            for j in range(max(i, k + 2), count)
        ]
        work += [functools.partial(solve, rows) for rows in strips]
        work += [
            functools.partial(subtract, rows, j)
            for j in range(k + 1, count)
            for rows in strips
        ]
        ahead = []
        if k + 2 == count:
            work.append(lambda: ahead.append(parts_of(rest[:, span(count - 1)])))
        inverse = factored(diagonal)
    last = count - 1
    finish(slice(0, nodes), last, exact_dot(ahead[0], parts_of(inverse), (1, 1)))
    for k in range(count):
        store(k).start()
    for k in range(count):
        store(k).wait()


def to_next(block, axis, distance):
    count = lax.axis_size(axis)
    return lax.ppermute(block, axis, [(i, (i + distance) % count) for i in range(count)])


def y_exchange(sent):
    if lax.axis_size("narrow") == 2:
        return to_next(sent, "narrow", 1)
    return jnp.concatenate(
        [to_next(sent[:1], "narrow", 1), to_next(sent[1:], "narrow", -1)]
    )


def on_device(orbitals, cell_matrix, cell_order):
    order_now = orbitals.shape[0]
    edge = order_now + 1
    width = orbitals.shape[3]
    box = f32(edge, edge, edge, width)
    plane, sent = f32(edge, edge, width), f32(edge * order_now, width)
    sums = (box, plane, plane, f32(2, edge, edge, width))
    cell_nodes = edge**3
    (matrix,) = vmem_call(
        permute_body,
        (jax.ShapeDtypeStruct((cell_nodes, cell_nodes), jnp.bfloat16),),
        flops=4 * cell_nodes**3,
    )(
        cell_matrix.reshape(cell_nodes, cell_nodes),
        cell_order.reshape(cell_nodes, 1),
    )

    x_next = to_next(orbitals[:1], "wide", -1)
    first_rows = jnp.concatenate([orbitals[:, :1], x_next[:, :1]], axis=0)
    y_next = to_next(first_rows, "narrow", -1)
    product_flops = 2 * cell_nodes**2 * width
    current, image, x_last, x_first, y_sent = vmem_call(
        first_body, (box, *sums), flops=product_flops
    )(orbitals, x_next, y_next, matrix)

    half_width = (band_high - band_low) / 2.0
    sigma_now = half_width / (anchor - (band_low + band_high) / 2.0)
    tau_value = 2.0 / sigma_now
    alpha, beta, previous = sigma_now / half_width, None, None
    for degree_step in range(1, DEG):
        y_faces = y_exchange(y_sent)
        (x_first,) = vmem_call(functools.partial(edge_body, at=0), (sent,))(
            x_first, y_faces
        )
        (x_last,) = vmem_call(functools.partial(edge_body, at=edge - 1), (sent,))(
            x_last, y_faces, x_first
        )
        x_high = to_next(x_first, "wide", -1)
        x_low = to_next(x_last, "wide", 1)
        operands = [image, y_faces, x_low, x_high, current]
        if previous is not None:
            operands.append(previous)
        if degree_step == DEG - 1:
            sums = (box, plane, f32(1, edge, edge, width))
        next_values, image, x_last, *rest, y_sent = vmem_call(
            functools.partial(middle_body, alpha=alpha, beta=beta),
            (box, *sums),
            scratch=[pltpu.VMEM(box.shape, jnp.float32)],
            flops=product_flops,
        )(*operands, matrix)
        previous, current = current, next_values
        x_first = rest[0] if rest else None
        sigma_new = 1.0 / (tau_value - sigma_now)
        alpha, beta = 2.0 * sigma_new / half_width, sigma_now * sigma_new
        sigma_now = sigma_new

    y_low = to_next(y_sent, "narrow", 1)
    (x_last,) = vmem_call(functools.partial(edge_body, at=edge - 1), (sent,))(
        x_last, y_low
    )
    x_low = to_next(x_last, "wide", 1)
    blocks = width // LANES
    rows = cut_rows(blocks * (blocks + 1) // 2 * LANES)
    first_stage = all_stages()[0]
    assert first_stage[2] == 2
    block_shape, half_shape = f32(order_now**2 * edge, width), f32(rows // 2, LANES)
    half_flops = 3 * cell_nodes * width**2
    stored, other = vmem_call(
        functools.partial(last_body, alpha=alpha, beta=beta),
        (block_shape, half_shape),
        scratch=[
            pltpu.VMEM(box.shape, jnp.float32),
            pltpu.VMEM(block_shape.shape, jnp.float32),
            pltpu.SemaphoreType.DMA,
        ],
        flops=half_flops,
        scalars=1,
        hbm_out=(0,),
    )(digit(first_stage), image, y_low, x_low, current, previous)
    (kept,) = vmem_call(
        kept_body,
        (half_shape,),
        scratch=[
            pltpu.VMEM(block_shape.shape, jnp.float32),
            pltpu.SemaphoreType.DMA,
        ],
        flops=half_flops,
        scalars=1,
        hbm_in=(1,),
    )(digit(first_stage), stored)

    nodes = order_now**3 * lax.axis_size("wide") * lax.axis_size("narrow")
    corr = summed(kept, other)
    (out,) = vmem_call(
        functools.partial(ortho_body, root_nodes=nodes**0.5),
        (f32(order_now**2, order_now, width),),
        scratch=[
            pltpu.VMEM((blocks * (blocks + 1) // 2, LANES, LANES), jnp.float32),
            pltpu.VMEM(block_shape.shape, jnp.float32),
            pltpu.VMEM((block_shape.shape[0], LANES), jnp.float32),
            pltpu.VMEM((blocks, order_now**2, order_now, LANES), jnp.float32),
            pltpu.SemaphoreType.DMA((blocks,)),
        ],
        flops=width**3,
        hbm_out=(0,),
    )(corr, stored)
    return out.reshape(orbitals.shape)


def solution(mesh):
    return jax.shard_map(
        on_device,
        mesh=mesh,
        in_specs=(
            P("wide", "narrow", None, None),
            P("wide", "narrow", None, None, None),
            P("wide", "narrow", None, None),
        ),
        out_specs=P("wide", "narrow", None, None),
        check_vma=False,
    )
```

```python
import functools

import jax
import jax.numpy as jnp
from jax import lax
from jax.experimental import pallas as pl
from jax.experimental.pallas import tpu as pltpu
from jax.sharding import PartitionSpec as P

DEG = 4
SUB = 8
LANES = 128
SLAB = 16
PARTS = 1
VMEM_LIMIT = 6 << 20


band_low = 4.0
band_high = 34.0
anchor = 0.0


def vmem_call(body, out_shapes, scratch=(), flops=0, scalars=0, hbm_in=(), hbm_out=()):
    def spec(in_hbm):
        return pl.BlockSpec(memory_space=pltpu.HBM if in_hbm else pltpu.VMEM)

    def call(*operands):
        operands = [
            x
            if n < scalars
            else pltpu.with_memory_space_constraint(
                x, pltpu.HBM if n in hbm_in else pltpu.VMEM
            )
            for n, x in enumerate(operands)
        ]
        outs = tuple(
            (pltpu.HBM if n in hbm_out else pltpu.VMEM)(x.shape, x.dtype)
            for n, x in enumerate(out_shapes)
        )
        return pl.pallas_call(
            body,
            out_shape=outs,
            in_specs=[pl.BlockSpec(memory_space=pltpu.SMEM)] * scalars
            + [spec(n in hbm_in) for n in range(scalars, len(operands))],
            out_specs=tuple(spec(n in hbm_out) for n in range(len(out_shapes))),
            scratch_shapes=list(scratch),
            compiler_params=pltpu.CompilerParams(vmem_limit_bytes=VMEM_LIMIT),
            cost_estimate=pl.CostEstimate(
                flops=flops, bytes_accessed=1 << 20, transcendentals=0
            ),
        )(*operands)

    return call


def f32(*shape):
    return jax.ShapeDtypeStruct(shape, jnp.float32)


def parts_of(x):
    high = x.astype(jnp.bfloat16)
    left = x - high.astype(jnp.float32)
    middle = left.astype(jnp.bfloat16)
    low = (left - middle.astype(jnp.float32)).astype(jnp.bfloat16)
    return high, middle, low


def exact_dot(a, b, dims=(1, 0)):
    (ah, am, al), (bh, bm, bl) = a, b
    return lax.dot_general(
        jnp.concatenate([ah, ah, am, am, ah, al], axis=dims[0]),
        jnp.concatenate([bh, bm, bh, bm, bl, bh], axis=dims[1]),
        (((dims[0],), (dims[1],)), ((), ())),
        preferred_element_type=jnp.float32,
    )


def permute_body(matrix, order, out):
    count = matrix.shape[0]
    pick = (
        lax.broadcasted_iota(jnp.int32, (count, count), 1) == order[...]
    ).astype(jnp.bfloat16)
    half = lax.dot_general(
        matrix[...],
        pick,
        (((1,), (0,)), ((), ())),
        preferred_element_type=jnp.float32,
    ).astype(jnp.bfloat16)
    out[...] = lax.dot_general(
        half, pick, (((0,), (0,)), ((), ())), preferred_element_type=jnp.float32
    ).astype(jnp.bfloat16)


def cell_product(values, matrix, image, *planes):
    edge = values.shape[0]
    width = values.shape[3]
    rows = values.reshape(edge**3, width).astype(jnp.bfloat16)
    products = jnp.dot(matrix[...], rows, preferred_element_type=jnp.float32)
    products = products.reshape(edge, edge, edge, width)
    wrap = products[:, :, :1] + products[:, :, edge - 1 :]
    where = lax.broadcasted_iota(jnp.int32, products.shape, 2)
    products = jnp.where((where == 0) | (where == edge - 1), wrap, products)
    image[...] = products
    x_last, *x_first, y_sent = planes
    x_last[...] = products[edge - 1]
    y_sent[0] = products[:, edge - 1]
    if x_first:
        x_first[0][...] = products[0]
        y_sent[1] = products[:, 0]


def first_body(own, x_next, y_next, matrix, values, *sums):
    order_now = own.shape[0]
    values[:order_now, :order_now, :order_now] = own[...]
    values[order_now:, :order_now, :order_now] = x_next[...]
    values[:, order_now:, :order_now] = y_next[...]
    values[:, :, order_now:] = values[:, :, :1]
    cell_product(values[...], matrix, *sums)


def edge_body(plane, y_faces, *refs, at):
    out = refs[-1]
    edge = plane.shape[0]
    order_now = edge - 1
    for b in range(edge):
        row = plane[b]
        if b == 0:
            row = row + y_faces[0, at]
        if b == edge - 1 and y_faces.shape[0] > 1:
            row = row + y_faces[1, at]
        out[order_now * b : order_now * (b + 1)] = row[:order_now]


def updated(image, y_faces, x_low, x_high, current, previous, alpha, beta):
    center = (band_low + band_high) / 2.0
    edge = image.shape[0]
    image[:, 0] = image[:, 0] + y_faces[0]
    if y_faces.shape[0] > 1:
        image[:, edge - 1] = image[:, edge - 1] + y_faces[1]
    order_now = edge - 1
    for at, got in ((0, x_low), (edge - 1, x_high)):
        if got is not None:
            for b in range(edge):
                first = order_now * b
                image[at, b, :order_now] += got[first : first + order_now]
                image[at, b, order_now:] += got[first : first + 1]
    got = (image[...] - center * current[...]) * alpha
    if previous is not None:
        got = got - beta * previous[...]
    return got


def middle_body(*refs, alpha, beta):
    if beta is None:
        image_in, y_faces, x_low, x_high, current, matrix, values, *sums, work = refs
        previous = None
    else:
        image_in, y_faces, x_low, x_high, current, previous, matrix, values, *sums, work = refs
    work[...] = image_in[...]
    got = updated(work, y_faces, x_low, x_high, current, previous, alpha, beta)
    values[...] = got
    cell_product(got, matrix, *sums)


def block_places(count, half_rows):
    pairs = [(i, j) for i in range(count) for j in range(i, count)]
    size = -(-len(pairs) // 2)
    return {
        pair: n // size * half_rows + n % size * LANES for n, pair in enumerate(pairs)
    }


def half_correlation(which, values, out, sofar=None):
    width = values.shape[1]
    half_rows = out.shape[0]
    high = values.astype(jnp.bfloat16)
    low = (values - high.astype(jnp.float32)).astype(jnp.bfloat16)

    def product(a, b):
        return lax.dot_general(
            a, b, (((0,), (0,)), ((), ())), preferred_element_type=jnp.float32
        )

    strips = {}
    for (i, j), at in block_places(width // LANES, half_rows).items():
        if at // half_rows == which:
            strips.setdefault(i, []).append((j, at - which * half_rows))
    for i, found in strips.items():
        rows = slice(i * LANES, (i + 1) * LANES)
        cols = slice(found[0][0] * LANES, (found[-1][0] + 1) * LANES)
        strip = (
            product(high[:, rows], low[:, cols]) + product(low[:, rows], high[:, cols])
        ) + product(high[:, rows], high[:, cols])
        for n, (_, at) in enumerate(found):
            block = strip[:, n * LANES : (n + 1) * LANES]
            if sofar is not None:
                block = block + sofar[at : at + LANES]
            out[at : at + LANES] = block


def chosen_half(number, values, out, sofar=None):
    for which in range(2):

        @pl.when(number == which)
        def _():
            half_correlation(which, values[...], out, sofar)


def last_planes(image, x_low, current, previous, y_face, planes, alpha, beta):
    center = (band_low + band_high) / 2.0
    order_now = image.shape[0] - 1
    width = image.shape[3]
    rows = []
    for a in planes:
        summed_up = image[a, :order_now]
        first = summed_up[:1] + y_face[0, a][None]
        if a == 0:
            first = first + spread_plane(x_low, 0, order_now)[None]
            others = [
                summed_up[b : b + 1] + spread_plane(x_low, b, order_now)[None]
                for b in range(1, order_now)
            ]
            summed_up = jnp.concatenate([first] + others, axis=0)
        else:
            summed_up = jnp.concatenate([first, summed_up[1:]], axis=0)
        got = (summed_up - center * current[a, :order_now]) * alpha
        got = got - beta * previous[a, :order_now]
        where = lax.broadcasted_iota(jnp.int32, got.shape, 1)
        got = jnp.where(where == order_now, 0.0, got)
        rows.append(got.reshape(order_now * (order_now + 1), width))
    return rows


def spread_plane(received, b, order_now):
    first = order_now * b
    return jnp.concatenate(
        [received[first : first + order_now], received[first : first + 1]], axis=0
    )


def inner_body(mine, image, y_face, current, previous, stored, other, kept, own, sem, *, alpha, beta):
    edge = image.shape[0]
    planes = range(1, edge - 1)
    found = last_planes(image, None, current, previous, y_face, planes, alpha, beta)
    own[...] = jnp.concatenate(found, axis=0)
    keep = pltpu.make_async_copy(own, stored, sem)
    keep.start()
    chosen_half(1 - mine[0], own, other)
    chosen_half(mine[0], own, kept)
    keep.wait()


def last_body(mine, image, y_face, x_low, current, previous, sofar, own, other, *, alpha, beta):
    (found,) = last_planes(image, x_low, current, previous, y_face, (0,), alpha, beta)
    own[...] = found
    chosen_half(1 - mine[0], own, other, sofar)


def kept_body(mine, own, sofar, kept):
    chosen_half(mine[0], own, kept, sofar)


def swap(block, axis, distance):
    count = lax.axis_size(axis)
    return lax.ppermute(block, axis, [(i, i ^ distance) for i in range(count)])


def stages_of(axis, size):
    stages, stride = [], 1
    while stride < size:
        radix = 2 if axis == "narrow" and stride == 1 else 4
        radix = min(radix, size // stride)
        stages.append((axis, stride, radix))
        stride *= radix
    return stages


def all_stages():
    return stages_of("narrow", lax.axis_size("narrow")) + stages_of(
        "wide", lax.axis_size("wide")
    )


def cut_rows(rows):
    cut = SUB
    for _, _, radix in all_stages()[:-1]:
        cut *= radix
    return -(-rows // cut) * cut


def cut_body(mine, *refs, count):
    terms, (*parts, work) = refs[:count], refs[count:]
    got = terms[0][...]
    for term in terms[1:]:
        got = got + term[...]
    work[...] = got
    rows = parts[0].shape[0]
    for d, part in enumerate(parts):
        part[...] = work[pl.ds(pl.multiple_of((mine[0] ^ d) * rows, SUB), rows)]


def digit(stage):
    axis, stride, radix = stage
    return (lax.axis_index(axis) // stride % radix).astype(jnp.int32)[None]


def summed(kept, other):
    lanes = kept.shape[1]
    stages = all_stages()
    parts = [kept, other]
    for stage, after in zip(stages[:-1], stages[1:]):
        axis, stride, _ = stage
        terms = [parts[0]] + [
            swap(parts[d], axis, d * stride) for d in reversed(range(1, len(parts)))
        ]
        rows, radix = terms[0].shape[0], after[2]
        if after == stages[-1]:
            radix = 1
        parts = vmem_call(
            functools.partial(cut_body, count=len(terms)),
            (f32(rows // radix, lanes),) * radix,
            scratch=[pltpu.VMEM((rows, lanes), jnp.float32)],
            scalars=1,
        )(digit(after) if radix > 1 else jnp.zeros((1,), jnp.int32), *terms)
    block = parts[0]
    axis, stride, radix = stages[-1]
    got = [swap(block, axis, d * stride) for d in reversed(range(1, radix))]
    got = [block] + got[::-1]
    while len(got) > 1:
        got = [a + b for a, b in zip(got[::2], got[1::2])]
    block = got[0]
    for axis, stride, radix in reversed(stages[:-1]):
        mine = lax.axis_index(axis) // stride % radix
        parts = jnp.zeros((radix,) + block.shape, block.dtype)
        parts = lax.dynamic_update_index_in_dim(parts, block, mine, 0)
        for d in reversed(range(1, radix)):
            parts = lax.dynamic_update_index_in_dim(
                parts, swap(block, axis, d * stride), mine ^ d, 0
            )
        block = parts.reshape(-1, lanes)
    return block


def lane_spread(tile, column):
    return jnp.broadcast_to(tile[:, column : column + 1], tile.shape)


def row_spread(tile, row):
    return jnp.broadcast_to(tile[row : row + 1, :], tile.shape)


def total(terms):
    while len(terms) > 1:
        terms = [a + b for a, b in zip(terms[::2], terms[1::2])]
    return terms[0]


def inverse_factor(block):
    size = block.shape[0]
    steps, per = size // SUB, SLAB // SUB
    tiles = [block[SUB * t : SUB * (t + 1)] for t in range(steps)]
    rows = lax.broadcasted_iota(jnp.int32, (SUB, size), 0)
    cols = lax.broadcasted_iota(jnp.int32, (SUB, size), 1)
    done = [None] * steps
    for s in range(0, steps, per):
        base = SUB * s
        own = (cols >= base) & (cols < base + SLAB)
        col = [
            {
                t: lane_spread(tiles[t], base + d)
                for t in range(s, s + per)
                if SUB * (t - s + 1) > d
            }
            for d in range(SLAB)
        ]
        before = list(tiles)
        for t in range(s, s + per):
            unit = jnp.where(cols == rows + SUB * t, 1.0, 0.0)
            tiles[t] = jnp.where(own, unit, tiles[t])
        for t in range(s + per, steps):
            tiles[t] = jnp.where(own, 0.0, tiles[t])

        def at(column, r):
            return row_spread(column[s + r // SUB], r % SUB)

        low, scale = [], []
        for k in range(0, SLAB, 2):
            x, y = col[k], col[k + 1]
            a, b, c = at(x, k), at(x, k + 1), at(y, k + 1)
            root = lax.rsqrt(a)
            next_root = lax.rsqrt(a * c - b * b)
            over = next_root * next_root
            p, q, u = {}, {}, {}
            for t in y:
                u[t] = a * y[t] - b * x[t]
                p[t] = (c * x[t] - b * y[t]) * over
                q[t] = u[t] * over
            for d in range(k + 2, SLAB):
                xd, yd = at(x, d), at(y, d)
                for t in col[d]:
                    col[d][t] = col[d][t] - (p[t] * xd + q[t] * yd)
            both = root * next_root
            here, r = s + k // SUB, k % SUB
            first = row_spread(tiles[here], r)
            second = row_spread(tiles[here], r + 1)
            for t in y:
                pm, qm = p[t], q[t]
                if t == here:
                    ratio = jnp.where(rows == r + 1, b * (root * root), 0.0)
                    pm = jnp.where(rows > r + 1, pm, ratio)
                    qm = jnp.where(rows > r + 1, qm, 0.0)
                tiles[t] = tiles[t] - (pm * first + qm * second)
            low.append({t: x[t] * root for t in y})
            low.append({t: u[t] * both for t in y})
            scale += [root, a * both]
        upper = []
        for i in range(per):
            t = s + i
            factors = scale[SUB * i]
            for k in range(1, SUB):
                factors = jnp.where(rows == k, scale[SUB * i + k], factors)
            tiles[t] = tiles[t] * factors
            done[t] = jnp.where(cols < base + SLAB, tiles[t], 0.0)
            upper += [row_spread(tiles[t], k) for k in range(SUB)]
        yield None
        if s + per < steps:
            solved = [None] * SLAB
            for k in reversed(range(SLAB)):
                row = upper[k]
                for m in reversed(range(k + 1, SLAB)):
                    row = row - at(low[k], m) * solved[m]
                solved[k] = row * scale[k]
            for t in range(s + per, steps):
                tiles[t] = tiles[t] - total(
                    [
                        lane_spread(before[t], base + k) * solved[k]
                        for k in reversed(range(SLAB))
                    ]
                )
    yield jnp.concatenate(done, axis=0)


def ortho_body(corr, first, inner, out, blocks, rest, done, sent, sems, *, root_nodes):
    width = first.shape[1]
    count = width // LANES
    plane = first.shape[0]
    nodes = plane + inner.shape[0]
    part = nodes // PARTS

    def span(k):
        return pl.ds(LANES * k, LANES)

    work = []

    def factored(block):
        share = -(-len(work) // (LANES // SLAB - 1))
        for got in inverse_factor(block):
            if got is None:
                for task in [work.pop(0) for _ in range(min(share, len(work)))]:
                    task()
        while work:
            work.pop(0)()
        return got

    rows_of = block_places(count, corr.shape[0] // 2)
    place = {pair: n for n, pair in enumerate(rows_of)}

    on_diagonal = lax.broadcasted_iota(
        jnp.int32, (LANES, LANES), 0
    ) == lax.broadcasted_iota(jnp.int32, (LANES, LANES), 1)
    over_row, over_col = [], []
    for i in range(count):
        at = rows_of[i, i]
        kept = jnp.where(on_diagonal, corr[at : at + LANES], 0.0)
        over_row.append(lax.rsqrt(jnp.sum(kept, axis=1, keepdims=True)))
        over_col.append(lax.rsqrt(jnp.sum(kept, axis=0, keepdims=True)))

    def piece(i, j):
        at = rows_of[i, j]
        return corr[at : at + LANES] * over_row[i] * over_col[j]

    def set_up():
        for (i, j), n in place.items():
            if j > 0:
                blocks[n] = piece(i, j)
        for j in range(count):
            over = over_col[j] * root_nodes
            rest[:plane, span(j)] = first[:, span(j)] * over
            rest[plane:, span(j)] = inner[:, span(j)] * over

    def store(k):
        return pltpu.make_async_copy(sent.at[k], out.at[:, :, span(k)], sems.at[k])

    def finish(rows, k, block):
        done[rows, :] = block
        first, last = rows.start // SUB, rows.stop // SUB
        shaped = block.reshape(last - first, SUB, LANES)
        sent[k, first:last] = shaped[:, : SUB - 1]

    work.append(set_up)
    inverse = factored(piece(0, 0))
    for k in range(count - 1):
        inverse = parts_of(inverse)
        near = parts_of(exact_dot(inverse, parts_of(blocks[place[k, k + 1]])))
        diagonal = blocks[place[k + 1, k + 1]] - exact_dot(near, near, (0, 0))
        ups = {k + 1: near}

        def up_of(j, k=k, inverse=inverse, ups=ups):
            ups[j] = parts_of(exact_dot(inverse, parts_of(blocks[place[k, j]])))

        def update(i, j, ups=ups):
            n = place[i, j]
            blocks[n] = blocks[n] - exact_dot(ups[i], ups[j], (0, 0))

        def solve(rows, k=k, inverse=inverse):
            finish(rows, k, exact_dot(parts_of(rest[rows, span(k)]), inverse, (1, 1)))

        def subtract(rows, j, ups=ups):
            step = exact_dot(parts_of(done[rows, :]), ups[j])
            rest[rows, span(j)] = rest[rows, span(j)] - step

        strips = [slice(r, r + part) for r in range(0, nodes, part)]
        later = range(k + 2, count)
        work += [functools.partial(up_of, j) for j in later]
        work += [
            functools.partial(update, i, j)
            for i in range(k + 1, count)
            for j in range(max(i, k + 2), count)
        ]
        work += [functools.partial(solve, rows) for rows in strips]
        work += [
            functools.partial(subtract, rows, j)
            for j in range(k + 1, count)
            for rows in strips
        ]
        ahead = []
        if k + 2 == count:
            work.append(lambda: ahead.append(parts_of(rest[:, span(count - 1)])))
        inverse = factored(diagonal)
    last = count - 1
    finish(slice(0, nodes), last, exact_dot(ahead[0], parts_of(inverse), (1, 1)))
    for k in range(count):
        store(k).start()
    for k in range(count):
        store(k).wait()


def to_next(block, axis, distance):
    count = lax.axis_size(axis)
    return lax.ppermute(block, axis, [(i, (i + distance) % count) for i in range(count)])


def y_exchange(sent):
    if lax.axis_size("narrow") == 2:
        return to_next(sent, "narrow", 1)
    return jnp.concatenate(
        [to_next(sent[:1], "narrow", 1), to_next(sent[1:], "narrow", -1)]
    )


def on_device(orbitals, cell_matrix, cell_order):
    order_now = orbitals.shape[0]
    edge = order_now + 1
    width = orbitals.shape[3]
    box = f32(edge, edge, edge, width)
    plane, sent = f32(edge, edge, width), f32(edge * order_now, width)
    sums = (box, plane, plane, f32(2, edge, edge, width))
    cell_nodes = edge**3
    (matrix,) = vmem_call(
        permute_body,
        (jax.ShapeDtypeStruct((cell_nodes, cell_nodes), jnp.bfloat16),),
        flops=4 * cell_nodes**3,
    )(
        cell_matrix.reshape(cell_nodes, cell_nodes),
        cell_order.reshape(cell_nodes, 1),
    )

    x_next = to_next(orbitals[:1], "wide", -1)
    first_rows = jnp.concatenate([orbitals[:, :1], x_next[:, :1]], axis=0)
    y_next = to_next(first_rows, "narrow", -1)
    product_flops = 2 * cell_nodes**2 * width
    current, image, x_last, x_first, y_sent = vmem_call(
        first_body, (box, *sums), flops=product_flops
    )(orbitals, x_next, y_next, matrix)

    half_width = (band_high - band_low) / 2.0
    sigma_now = half_width / (anchor - (band_low + band_high) / 2.0)
    tau_value = 2.0 / sigma_now
    alpha, beta, previous = sigma_now / half_width, None, None
    for degree_step in range(1, DEG):
        y_faces = y_exchange(y_sent)
        (x_first,) = vmem_call(functools.partial(edge_body, at=0), (sent,))(
            x_first, y_faces
        )
        (x_last,) = vmem_call(functools.partial(edge_body, at=edge - 1), (sent,))(
            x_last, y_faces, x_first
        )
        x_high = to_next(x_first, "wide", -1)
        x_low = to_next(x_last, "wide", 1)
        operands = [image, y_faces, x_low, x_high, current]
        if previous is not None:
            operands.append(previous)
        if degree_step == DEG - 1:
            sums = (box, plane, f32(1, edge, edge, width))
        next_values, image, x_last, *rest, y_sent = vmem_call(
            functools.partial(middle_body, alpha=alpha, beta=beta),
            (box, *sums),
            scratch=[pltpu.VMEM(box.shape, jnp.float32)],
            flops=product_flops,
        )(*operands, matrix)
        previous, current = current, next_values
        x_first = rest[0] if rest else None
        sigma_new = 1.0 / (tau_value - sigma_now)
        alpha, beta = 2.0 * sigma_new / half_width, sigma_now * sigma_new
        sigma_now = sigma_new

    y_low = to_next(y_sent, "narrow", 1)
    (x_last,) = vmem_call(functools.partial(edge_body, at=edge - 1), (sent,))(
        x_last, y_low
    )
    x_low = to_next(x_last, "wide", 1)
    blocks = width // LANES
    rows = cut_rows(blocks * (blocks + 1) // 2 * LANES)
    first_stage = all_stages()[0]
    assert first_stage[2] == 2
    plane_rows = order_now * edge
    inner_shape = f32((order_now - 1) * plane_rows, width)
    half_shape = f32(rows // 2, LANES)
    stored, other, kept = vmem_call(
        functools.partial(inner_body, alpha=alpha, beta=beta),
        (inner_shape, half_shape, half_shape),
        scratch=[
            pltpu.VMEM(inner_shape.shape, jnp.float32),
            pltpu.SemaphoreType.DMA,
        ],
        flops=6 * cell_nodes * width**2,
        scalars=1,
        hbm_out=(0,),
    )(digit(first_stage), image, y_low, current, previous)
    own, other = vmem_call(
        functools.partial(last_body, alpha=alpha, beta=beta),
        (f32(plane_rows, width), half_shape),
        flops=6 * plane_rows * width**2,
        scalars=1,
    )(digit(first_stage), image, y_low, x_low, current, previous, other)
    (kept,) = vmem_call(
        kept_body, (half_shape,), flops=6 * plane_rows * width**2, scalars=1
    )(digit(first_stage), own, kept)

    nodes = order_now**3 * lax.axis_size("wide") * lax.axis_size("narrow")
    corr = summed(kept, other)
    (out,) = vmem_call(
        functools.partial(ortho_body, root_nodes=nodes**0.5),
        (f32(order_now**2, order_now, width),),
        scratch=[
            pltpu.VMEM((blocks * (blocks + 1) // 2, LANES, LANES), jnp.float32),
            pltpu.VMEM((order_now * plane_rows, width), jnp.float32),
            pltpu.VMEM((order_now * plane_rows, LANES), jnp.float32),
            pltpu.VMEM((blocks, order_now**2, order_now, LANES), jnp.float32),
            pltpu.SemaphoreType.DMA((blocks,)),
        ],
        flops=width**3,
        hbm_out=(0,),
    )(corr, own, stored)
    return out.reshape(orbitals.shape)


def solution(mesh):
    return jax.shard_map(
        on_device,
        mesh=mesh,
        in_specs=(
            P("wide", "narrow", None, None),
            P("wide", "narrow", None, None, None),
            P("wide", "narrow", None, None),
        ),
        out_specs=P("wide", "narrow", None, None),
        check_vma=False,
    )
```

```python
import functools

import jax
import jax.numpy as jnp
from jax import lax
from jax.experimental import pallas as pl
from jax.experimental.pallas import tpu as pltpu
from jax.sharding import PartitionSpec as P

DEG = 4
SUB = 8
LANES = 128
SLAB = 16
PARTS = 1
VMEM_LIMIT = 6 << 20


band_low = 4.0
band_high = 34.0
anchor = 0.0


def vmem_call(body, out_shapes, scratch=(), flops=0, scalars=0, hbm_in=(), hbm_out=()):
    def spec(in_hbm):
        return pl.BlockSpec(memory_space=pltpu.HBM if in_hbm else pltpu.VMEM)

    def call(*operands):
        operands = [
            x
            if n < scalars
            else pltpu.with_memory_space_constraint(
                x, pltpu.HBM if n in hbm_in else pltpu.VMEM
            )
            for n, x in enumerate(operands)
        ]
        outs = tuple(
            (pltpu.HBM if n in hbm_out else pltpu.VMEM)(x.shape, x.dtype)
            for n, x in enumerate(out_shapes)
        )
        return pl.pallas_call(
            body,
            out_shape=outs,
            in_specs=[pl.BlockSpec(memory_space=pltpu.SMEM)] * scalars
            + [spec(n in hbm_in) for n in range(scalars, len(operands))],
            out_specs=tuple(spec(n in hbm_out) for n in range(len(out_shapes))),
            scratch_shapes=list(scratch),
            compiler_params=pltpu.CompilerParams(vmem_limit_bytes=VMEM_LIMIT),
            cost_estimate=pl.CostEstimate(
                flops=flops, bytes_accessed=1 << 20, transcendentals=0
            ),
        )(*operands)

    return call


def f32(*shape):
    return jax.ShapeDtypeStruct(shape, jnp.float32)


def parts_of(x):
    high = x.astype(jnp.bfloat16)
    left = x - high.astype(jnp.float32)
    middle = left.astype(jnp.bfloat16)
    low = (left - middle.astype(jnp.float32)).astype(jnp.bfloat16)
    return high, middle, low


def exact_dot(a, b, dims=(1, 0)):
    (ah, am, al), (bh, bm, bl) = a, b
    return lax.dot_general(
        jnp.concatenate([ah, ah, am, am, ah, al], axis=dims[0]),
        jnp.concatenate([bh, bm, bh, bm, bl, bh], axis=dims[1]),
        (((dims[0],), (dims[1],)), ((), ())),
        preferred_element_type=jnp.float32,
    )


def permute_body(matrix, order, out):
    count = matrix.shape[0]
    pick = (
        lax.broadcasted_iota(jnp.int32, (count, count), 1) == order[...]
    ).astype(jnp.bfloat16)
    half = lax.dot_general(
        matrix[...],
        pick,
        (((1,), (0,)), ((), ())),
        preferred_element_type=jnp.float32,
    ).astype(jnp.bfloat16)
    out[...] = lax.dot_general(
        half, pick, (((0,), (0,)), ((), ())), preferred_element_type=jnp.float32
    ).astype(jnp.bfloat16)


def cell_product(values, matrix, image, *planes):
    edge = values.shape[0]
    width = values.shape[3]
    rows = values.reshape(edge**3, width).astype(jnp.bfloat16)
    products = jnp.dot(matrix[...], rows, preferred_element_type=jnp.float32)
    products = products.reshape(edge, edge, edge, width)
    wrap = products[:, :, :1] + products[:, :, edge - 1 :]
    where = lax.broadcasted_iota(jnp.int32, products.shape, 2)
    products = jnp.where((where == 0) | (where == edge - 1), wrap, products)
    image[...] = products
    x_last, *x_first, y_sent = planes
    x_last[...] = products[edge - 1]
    y_sent[0] = products[:, edge - 1]
    if x_first:
        x_first[0][...] = products[0]
        y_sent[1] = products[:, 0]


def first_body(own, x_next, y_next, matrix, values, *sums):
    order_now = own.shape[0]
    values[:order_now, :order_now, :order_now] = own[...]
    values[order_now:, :order_now, :order_now] = x_next[...]
    values[:, order_now:, :order_now] = y_next[...]
    values[:, :, order_now:] = values[:, :, :1]
    cell_product(values[...], matrix, *sums)


def edge_body(plane, y_faces, *refs, at):
    out = refs[-1]
    edge = plane.shape[0]
    order_now = edge - 1
    for b in range(edge):
        row = plane[b]
        if b == 0:
            row = row + y_faces[0, at]
        if b == edge - 1 and y_faces.shape[0] > 1:
            row = row + y_faces[1, at]
        out[order_now * b : order_now * (b + 1)] = row[:order_now]


def updated(image, y_faces, x_low, x_high, current, previous, alpha, beta):
    center = (band_low + band_high) / 2.0
    edge = image.shape[0]
    image[:, 0] = image[:, 0] + y_faces[0]
    if y_faces.shape[0] > 1:
        image[:, edge - 1] = image[:, edge - 1] + y_faces[1]
    order_now = edge - 1
    for at, got in ((0, x_low), (edge - 1, x_high)):
        if got is not None:
            for b in range(edge):
                first = order_now * b
                image[at, b, :order_now] += got[first : first + order_now]
                image[at, b, order_now:] += got[first : first + 1]
    got = (image[...] - center * current[...]) * alpha
    if previous is not None:
        got = got - beta * previous[...]
    return got


def middle_body(*refs, alpha, beta):
    if beta is None:
        image_in, y_faces, x_low, x_high, current, matrix, values, *sums, work = refs
        previous = None
    else:
        image_in, y_faces, x_low, x_high, current, previous, matrix, values, *sums, work = refs
    work[...] = image_in[...]
    got = updated(work, y_faces, x_low, x_high, current, previous, alpha, beta)
    values[...] = got
    cell_product(got, matrix, *sums)


def block_places(count, half_rows):
    pairs = [(i, j) for i in range(count) for j in range(i, count)]
    size = -(-len(pairs) // 2)
    return {
        pair: n // size * half_rows + n % size * LANES for n, pair in enumerate(pairs)
    }


def half_correlation(which, values, out, sofar=None):
    width = values.shape[1]
    half_rows = out.shape[0]
    high = values.astype(jnp.bfloat16)
    low = (values - high.astype(jnp.float32)).astype(jnp.bfloat16)

    def product(a, b):
        return lax.dot_general(
            a, b, (((0,), (0,)), ((), ())), preferred_element_type=jnp.float32
        )

    strips = {}
    for (i, j), at in block_places(width // LANES, half_rows).items():
        if at // half_rows == which:
            strips.setdefault(i, []).append((j, at - which * half_rows))
    for i, found in strips.items():
        rows = slice(i * LANES, (i + 1) * LANES)
        cols = slice(found[0][0] * LANES, (found[-1][0] + 1) * LANES)
        strip = (
            product(high[:, rows], low[:, cols]) + product(low[:, rows], high[:, cols])
        ) + product(high[:, rows], high[:, cols])
        for n, (_, at) in enumerate(found):
            block = strip[:, n * LANES : (n + 1) * LANES]
            if sofar is not None:
                block = block + sofar[at : at + LANES]
            out[at : at + LANES] = block


def chosen_half(number, values, out, sofar=None):
    for which in range(2):

        @pl.when(number == which)
        def _():
            half_correlation(which, values[...], out, sofar)


def last_planes(image, x_low, current, previous, y_face, planes, alpha, beta):
    center = (band_low + band_high) / 2.0
    order_now = image.shape[0] - 1
    width = image.shape[3]
    rows = []
    for a in planes:
        summed_up = image[a, :order_now]
        first = summed_up[:1] + y_face[0, a][None]
        if a == 0:
            first = first + spread_plane(x_low, 0, order_now)[None]
            others = [
                summed_up[b : b + 1] + spread_plane(x_low, b, order_now)[None]
                for b in range(1, order_now)
            ]
            summed_up = jnp.concatenate([first] + others, axis=0)
        else:
            summed_up = jnp.concatenate([first, summed_up[1:]], axis=0)
        got = (summed_up - center * current[a, :order_now]) * alpha
        got = got - beta * previous[a, :order_now]
        where = lax.broadcasted_iota(jnp.int32, got.shape, 1)
        got = jnp.where(where == order_now, 0.0, got)
        rows.append(got.reshape(order_now * (order_now + 1), width))
    return rows


def spread_plane(received, b, order_now):
    first = order_now * b
    return jnp.concatenate(
        [received[first : first + order_now], received[first : first + 1]], axis=0
    )


def inner_body(mine, image, y_face, current, previous, stored, other, kept, own, sem, *, alpha, beta):
    edge = image.shape[0]
    planes = range(1, edge - 1)
    found = last_planes(image, None, current, previous, y_face, planes, alpha, beta)
    own[...] = jnp.concatenate(found, axis=0)
    keep = pltpu.make_async_copy(own, stored, sem)
    keep.start()
    chosen_half(1 - mine[0], own, other)
    chosen_half(mine[0], own, kept)
    keep.wait()


def last_body(mine, image, y_face, x_low, current, previous, sofar, own, other, *, alpha, beta):
    (found,) = last_planes(image, x_low, current, previous, y_face, (0,), alpha, beta)
    own[...] = found
    chosen_half(1 - mine[0], own, other, sofar)


def kept_body(mine, own, sofar, kept):
    chosen_half(mine[0], own, kept, sofar)


def swap(block, axis, distance):
    count = lax.axis_size(axis)
    return lax.ppermute(block, axis, [(i, i ^ distance) for i in range(count)])


def stages_of(axis, size):
    stages, stride = [], 1
    while stride < size:
        radix = 2 if axis == "narrow" and stride == 1 else 4
        radix = min(radix, size // stride)
        stages.append((axis, stride, radix))
        stride *= radix
    return stages


def all_stages():
    return stages_of("narrow", lax.axis_size("narrow")) + stages_of(
        "wide", lax.axis_size("wide")
    )


def cut_rows(rows):
    cut = SUB
    for _, _, radix in all_stages()[:-1]:
        cut *= radix
    return -(-rows // cut) * cut


def cut_body(mine, *refs, count):
    terms, (*parts, work) = refs[:count], refs[count:]
    got = terms[0][...]
    for term in terms[1:]:
        got = got + term[...]
    work[...] = got
    rows = parts[0].shape[0]
    for d, part in enumerate(parts):
        part[...] = work[pl.ds(pl.multiple_of((mine[0] ^ d) * rows, SUB), rows)]


def digit(stage):
    axis, stride, radix = stage
    return (lax.axis_index(axis) // stride % radix).astype(jnp.int32)[None]


def summed(kept, other):
    lanes = kept.shape[1]
    stages = all_stages()
    parts = [kept, other]
    for stage, after in zip(stages[:-1], stages[1:]):
        axis, stride, _ = stage
        terms = [parts[0]] + [
            swap(parts[d], axis, d * stride) for d in range(1, len(parts))
        ]
        rows, radix = terms[0].shape[0], after[2]
        if after == stages[-1]:
            radix = 1
        parts = vmem_call(
            functools.partial(cut_body, count=len(terms)),
            (f32(rows // radix, lanes),) * radix,
            scratch=[pltpu.VMEM((rows, lanes), jnp.float32)],
            scalars=1,
        )(digit(after) if radix > 1 else jnp.zeros((1,), jnp.int32), *terms)
    block = parts[0]
    axis, stride, radix = stages[-1]
    got = [swap(block, axis, d * stride) for d in reversed(range(1, radix))]
    got = [block] + got[::-1]
    while len(got) > 1:
        got = [a + b for a, b in zip(got[::2], got[1::2])]
    block = got[0]
    for axis, stride, radix in reversed(stages[:-1]):
        mine = lax.axis_index(axis) // stride % radix
        parts = jnp.zeros((radix,) + block.shape, block.dtype)
        parts = lax.dynamic_update_index_in_dim(parts, block, mine, 0)
        for d in reversed(range(1, radix)):
            parts = lax.dynamic_update_index_in_dim(
                parts, swap(block, axis, d * stride), mine ^ d, 0
            )
        block = parts.reshape(-1, lanes)
    return block


def lane_spread(tile, column):
    return jnp.broadcast_to(tile[:, column : column + 1], tile.shape)


def row_spread(tile, row):
    return jnp.broadcast_to(tile[row : row + 1, :], tile.shape)


def total(terms):
    while len(terms) > 1:
        terms = [a + b for a, b in zip(terms[::2], terms[1::2])]
    return terms[0]


def inverse_factor(block):
    size = block.shape[0]
    steps, per = size // SUB, SLAB // SUB
    tiles = [block[SUB * t : SUB * (t + 1)] for t in range(steps)]
    rows = lax.broadcasted_iota(jnp.int32, (SUB, size), 0)
    cols = lax.broadcasted_iota(jnp.int32, (SUB, size), 1)
    done = [None] * steps
    for s in range(0, steps, per):
        base = SUB * s
        own = (cols >= base) & (cols < base + SLAB)
        col = [
            {
                t: lane_spread(tiles[t], base + d)
                for t in range(s, s + per)
                if SUB * (t - s + 1) > d
            }
            for d in range(SLAB)
        ]
        before = list(tiles)
        for t in range(s, s + per):
            unit = jnp.where(cols == rows + SUB * t, 1.0, 0.0)
            tiles[t] = jnp.where(own, unit, tiles[t])
        for t in range(s + per, steps):
            tiles[t] = jnp.where(own, 0.0, tiles[t])

        def at(column, r):
            return row_spread(column[s + r // SUB], r % SUB)

        low, scale = [], []
        for k in range(0, SLAB, 2):
            x, y = col[k], col[k + 1]
            a, b, c = at(x, k), at(x, k + 1), at(y, k + 1)
            root = lax.rsqrt(a)
            next_root = lax.rsqrt(a * c - b * b)
            over = next_root * next_root
            p, q, u = {}, {}, {}
            for t in y:
                u[t] = a * y[t] - b * x[t]
                p[t] = (c * x[t] - b * y[t]) * over
                q[t] = u[t] * over
            for d in range(k + 2, SLAB):
                xd, yd = at(x, d), at(y, d)
                for t in col[d]:
                    col[d][t] = col[d][t] - (p[t] * xd + q[t] * yd)
            both = root * next_root
            here, r = s + k // SUB, k % SUB
            first = row_spread(tiles[here], r)
            second = row_spread(tiles[here], r + 1)
            for t in y:
                pm, qm = p[t], q[t]
                if t == here:
                    ratio = jnp.where(rows == r + 1, b * (root * root), 0.0)
                    pm = jnp.where(rows > r + 1, pm, ratio)
                    qm = jnp.where(rows > r + 1, qm, 0.0)
                tiles[t] = tiles[t] - (pm * first + qm * second)
            low.append({t: x[t] * root for t in y})
            low.append({t: u[t] * both for t in y})
            scale += [root, a * both]
        upper = []
        for i in range(per):
            t = s + i
            factors = scale[SUB * i]
            for k in range(1, SUB):
                factors = jnp.where(rows == k, scale[SUB * i + k], factors)
            tiles[t] = tiles[t] * factors
            done[t] = jnp.where(cols < base + SLAB, tiles[t], 0.0)
            upper += [row_spread(tiles[t], k) for k in range(SUB)]
        yield None
        if s + per < steps:
            solved = [None] * SLAB
            for k in reversed(range(SLAB)):
                row = upper[k]
                for m in reversed(range(k + 1, SLAB)):
                    row = row - at(low[k], m) * solved[m]
                solved[k] = row * scale[k]
            for t in range(s + per, steps):
                tiles[t] = tiles[t] - total(
                    [
                        lane_spread(before[t], base + k) * solved[k]
                        for k in reversed(range(SLAB))
                    ]
                )
    yield jnp.concatenate(done, axis=0)


def ortho_body(corr, first, inner, out, blocks, rest, done, sent, sems, *, root_nodes):
    width = first.shape[1]
    count = width // LANES
    plane = first.shape[0]
    nodes = plane + inner.shape[0]
    part = nodes // PARTS

    def span(k):
        return pl.ds(LANES * k, LANES)

    work = []

    def factored(block):
        share = -(-len(work) // (LANES // SLAB - 1))
        for got in inverse_factor(block):
            if got is None:
                for task in [work.pop(0) for _ in range(min(share, len(work)))]:
                    task()
        while work:
            work.pop(0)()
        return got

    rows_of = block_places(count, corr.shape[0] // 2)
    place = {pair: n for n, pair in enumerate(rows_of)}

    on_diagonal = lax.broadcasted_iota(
        jnp.int32, (LANES, LANES), 0
    ) == lax.broadcasted_iota(jnp.int32, (LANES, LANES), 1)
    over_row, over_col = [], []
    for i in range(count):
        at = rows_of[i, i]
        kept = jnp.where(on_diagonal, corr[at : at + LANES], 0.0)
        over_row.append(lax.rsqrt(jnp.sum(kept, axis=1, keepdims=True)))
        over_col.append(lax.rsqrt(jnp.sum(kept, axis=0, keepdims=True)))

    def piece(i, j):
        at = rows_of[i, j]
        return corr[at : at + LANES] * over_row[i] * over_col[j]

    def set_up():
        for (i, j), n in place.items():
            if j > 0:
                blocks[n] = piece(i, j)
        for j in range(count):
            over = over_col[j] * root_nodes
            rest[:plane, span(j)] = first[:, span(j)] * over
            rest[plane:, span(j)] = inner[:, span(j)] * over

    def store(k):
        return pltpu.make_async_copy(sent.at[k], out.at[:, :, span(k)], sems.at[k])

    def finish(rows, k, block):
        done[rows, :] = block
        first, last = rows.start // SUB, rows.stop // SUB
        shaped = block.reshape(last - first, SUB, LANES)
        sent[k, first:last] = shaped[:, : SUB - 1]

    work.append(set_up)
    inverse = factored(piece(0, 0))
    for k in range(count - 1):
        inverse = parts_of(inverse)
        near = parts_of(exact_dot(inverse, parts_of(blocks[place[k, k + 1]])))
        diagonal = blocks[place[k + 1, k + 1]] - exact_dot(near, near, (0, 0))
        ups = {k + 1: near}

        def up_of(j, k=k, inverse=inverse, ups=ups):
            ups[j] = parts_of(exact_dot(inverse, parts_of(blocks[place[k, j]])))

        def update(i, j, ups=ups):
            n = place[i, j]
            blocks[n] = blocks[n] - exact_dot(ups[i], ups[j], (0, 0))

        def solve(rows, k=k, inverse=inverse):
            finish(rows, k, exact_dot(parts_of(rest[rows, span(k)]), inverse, (1, 1)))

        def subtract(rows, j, ups=ups):
            step = exact_dot(parts_of(done[rows, :]), ups[j])
            rest[rows, span(j)] = rest[rows, span(j)] - step

        strips = [slice(r, r + part) for r in range(0, nodes, part)]
        later = range(k + 2, count)
        work += [functools.partial(up_of, j) for j in later]
        work += [
            functools.partial(update, i, j)
            for i in range(k + 1, count)
            for j in range(max(i, k + 2), count)
        ]
        work += [functools.partial(solve, rows) for rows in strips]
        work += [
            functools.partial(subtract, rows, j)
            for j in range(k + 1, count)
            for rows in strips
        ]
        ahead = []
        if k + 2 == count:
            work.append(lambda: ahead.append(parts_of(rest[:, span(count - 1)])))
        inverse = factored(diagonal)
    last = count - 1
    finish(slice(0, nodes), last, exact_dot(ahead[0], parts_of(inverse), (1, 1)))
    for k in range(count):
        store(k).start()
    for k in range(count):
        store(k).wait()


def to_next(block, axis, distance):
    count = lax.axis_size(axis)
    return lax.ppermute(block, axis, [(i, (i + distance) % count) for i in range(count)])


def y_exchange(sent):
    if lax.axis_size("narrow") == 2:
        return to_next(sent, "narrow", 1)
    return jnp.concatenate(
        [to_next(sent[:1], "narrow", 1), to_next(sent[1:], "narrow", -1)]
    )


def on_device(orbitals, cell_matrix, cell_order):
    order_now = orbitals.shape[0]
    edge = order_now + 1
    width = orbitals.shape[3]
    box = f32(edge, edge, edge, width)
    plane, sent = f32(edge, edge, width), f32(edge * order_now, width)
    sums = (box, plane, plane, f32(2, edge, edge, width))
    cell_nodes = edge**3
    (matrix,) = vmem_call(
        permute_body,
        (jax.ShapeDtypeStruct((cell_nodes, cell_nodes), jnp.bfloat16),),
        flops=4 * cell_nodes**3,
    )(
        cell_matrix.reshape(cell_nodes, cell_nodes),
        cell_order.reshape(cell_nodes, 1),
    )

    x_next = to_next(orbitals[:1], "wide", -1)
    first_rows = jnp.concatenate([orbitals[:, :1], x_next[:, :1]], axis=0)
    y_next = to_next(first_rows, "narrow", -1)
    product_flops = 2 * cell_nodes**2 * width
    current, image, x_last, x_first, y_sent = vmem_call(
        first_body, (box, *sums), flops=product_flops
    )(orbitals, x_next, y_next, matrix)

    half_width = (band_high - band_low) / 2.0
    sigma_now = half_width / (anchor - (band_low + band_high) / 2.0)
    tau_value = 2.0 / sigma_now
    alpha, beta, previous = sigma_now / half_width, None, None
    for degree_step in range(1, DEG):
        y_faces = y_exchange(y_sent)
        (x_first,) = vmem_call(functools.partial(edge_body, at=0), (sent,))(
            x_first, y_faces
        )
        (x_last,) = vmem_call(functools.partial(edge_body, at=edge - 1), (sent,))(
            x_last, y_faces, x_first
        )
        x_high = to_next(x_first, "wide", -1)
        x_low = to_next(x_last, "wide", 1)
        operands = [image, y_faces, x_low, x_high, current]
        if previous is not None:
            operands.append(previous)
        if degree_step == DEG - 1:
            sums = (box, plane, f32(1, edge, edge, width))
        next_values, image, x_last, *rest, y_sent = vmem_call(
            functools.partial(middle_body, alpha=alpha, beta=beta),
            (box, *sums),
            scratch=[pltpu.VMEM(box.shape, jnp.float32)],
            flops=product_flops,
        )(*operands, matrix)
        previous, current = current, next_values
        x_first = rest[0] if rest else None
        sigma_new = 1.0 / (tau_value - sigma_now)
        alpha, beta = 2.0 * sigma_new / half_width, sigma_now * sigma_new
        sigma_now = sigma_new

    y_low = to_next(y_sent, "narrow", 1)
    (x_last,) = vmem_call(functools.partial(edge_body, at=edge - 1), (sent,))(
        x_last, y_low
    )
    x_low = to_next(x_last, "wide", 1)
    blocks = width // LANES
    rows = cut_rows(blocks * (blocks + 1) // 2 * LANES)
    first_stage = all_stages()[0]
    assert first_stage[2] == 2
    plane_rows = order_now * edge
    inner_shape = f32((order_now - 1) * plane_rows, width)
    half_shape = f32(rows // 2, LANES)
    stored, other, kept = vmem_call(
        functools.partial(inner_body, alpha=alpha, beta=beta),
        (inner_shape, half_shape, half_shape),
        scratch=[
            pltpu.VMEM(inner_shape.shape, jnp.float32),
            pltpu.SemaphoreType.DMA,
        ],
        flops=6 * cell_nodes * width**2,
        scalars=1,
        hbm_out=(0,),
    )(digit(first_stage), image, y_low, current, previous)
    own, other = vmem_call(
        functools.partial(last_body, alpha=alpha, beta=beta),
        (f32(plane_rows, width), half_shape),
        flops=6 * plane_rows * width**2,
        scalars=1,
    )(digit(first_stage), image, y_low, x_low, current, previous, other)
    (kept,) = vmem_call(
        kept_body, (half_shape,), flops=6 * plane_rows * width**2, scalars=1
    )(digit(first_stage), own, kept)

    nodes = order_now**3 * lax.axis_size("wide") * lax.axis_size("narrow")
    corr = summed(kept, other)
    (out,) = vmem_call(
        functools.partial(ortho_body, root_nodes=nodes**0.5),
        (f32(order_now**2, order_now, width),),
        scratch=[
            pltpu.VMEM((blocks * (blocks + 1) // 2, LANES, LANES), jnp.float32),
            pltpu.VMEM((order_now * plane_rows, width), jnp.float32),
            pltpu.VMEM((order_now * plane_rows, LANES), jnp.float32),
            pltpu.VMEM((blocks, order_now**2, order_now, LANES), jnp.float32),
            pltpu.SemaphoreType.DMA((blocks,)),
        ],
        flops=width**3,
        hbm_out=(0,),
    )(corr, own, stored)
    return out.reshape(orbitals.shape)


def solution(mesh):
    return jax.shard_map(
        on_device,
        mesh=mesh,
        in_specs=(
            P("wide", "narrow", None, None),
            P("wide", "narrow", None, None, None),
            P("wide", "narrow", None, None),
        ),
        out_specs=P("wide", "narrow", None, None),
        check_vma=False,
    )
```
